512 devices in a mesh: dp: 16 (over z), ctx: 16 (over x_lo, y, core), head: 2 (over x_hi).
Axes of the slice: x: 4 (x_hi: 2, x_lo: 2; x = x_hi * 2 + x_lo), y: 4, z: 16, core: 2. Of those that a mesh axis runs over, the one named last changes fastest.
Arguments:
- queries: bfloat16 [32768, 4096], P(('dp', 'ctx'), 'head'), parts along dimension 0, may hold values from -18 to 18
- keys: bfloat16 [32768, 1024], P(('dp', 'ctx'), 'head'), parts along dimension 0, may hold values from -18 to 18
- values: bfloat16 [32768, 1024], P(('dp', 'ctx'), 'head'), parts along dimension 0, may hold values from -6 to 6
- doc_lengths: int32 [256], P('dp'), parts along dimension 0, may hold values from 1 to 1024, 2048 in all
- owner_map: int32 [256, 16], P('dp'), parts along dimension 0, may hold values from 0 to 15, each once within a row
Outputs:
- attended: bfloat16 [32768, 4096], P(('dp', 'ctx'), 'head'), parts along dimension 0
The draws below stay inside these ranges and needn't reach their ends.
There are 16 independent parts, one for each index of `dp`. The reference program is written for one: setup_inputs(seed, part) draws one part's arguments, and reference() takes and returns one part's arrays. A program takes and returns all parts, laid end to end along the dimension named above; each array names one. Nothing has to cross between parts.
Inputs may be any that keep to these rules, and one draw needn't show every extreme that they name: Each row of owner_map names every ctx index exactly once. `doc_lengths`: the lengths sum to 2048; the longest is exactly 1024.
All inputs are finite; a program needn't handle non-finite values.
Results may differ from the reference program's by a relative error of at most 0.003.
Values may be sent and summed in bfloat16 or wider, within the bound.
No kernel may reach another device: no remote copies, remote signals or barrier semaphores. Data moves between devices by JAX's collectives and lax.ppermute only.
A program may use at most 64 MiB of HBM per device.

```python
import math
import jax
import jax.numpy as jnp
import numpy as np
from jax import lax

QUERY_HEADS = 32
KEY_VALUE_HEADS = 8
HEAD_SIZE = 128
TOKENS_PER_SHARD = 128
NDOC = 16
CONTEXT_TOKENS = 2048
BR = 8
N_CTX = 16


def draw_queries(key, part):
    key = jax.random.fold_in(key, 1)
    base_offset = jnp.clip(jax.random.normal(key, (CONTEXT_TOKENS, QUERY_HEADS * HEAD_SIZE), jnp.float32), -3.5, 3.5)
    return base_offset.astype(jnp.bfloat16)


def draw_keys(key, part):
    key = jax.random.fold_in(key, 2)
    base_offset = jnp.clip(jax.random.normal(key, (CONTEXT_TOKENS, KEY_VALUE_HEADS * HEAD_SIZE), jnp.float32), -3.5, 3.5)
    return base_offset.astype(jnp.bfloat16)


def level_of(key, dims, shards, low, largest):
    def one(dim, shards_of):
        draws = jax.random.uniform(jax.random.fold_in(jax.random.fold_in(key, 6), dim), (shards_of,), jnp.float32, low / len(shards), largest / len(shards))
        return jnp.repeat(jnp.exp(draws), dims[dim] // shards_of).reshape((-1,) + (1,) * (len(dims) - dim - 1))

    gain = one(*shards[0])
    for cut in shards[1:]:
        gain = gain * one(*cut)
    return gain


def profile(count, total, most, slope):
    loads = [(1 << 20) // math.isqrt(rank ** slope) + 1 for rank in range(2, count + 1)]
    rest, given = total - most - (count - 1), [1] * (count - 1)
    while rest > 0:
        free = [i for i in range(count - 1) if given[i] < most]
        pool, remaining = sum([loads[i] for i in free]), rest
        for i in free:
            addition = min(most - given[i], max(1, remaining * loads[i] // pool), rest)
            given[i] = given[i] + addition
            rest = rest - addition
    return np.array([most] + given)


def uneven(rng, amount, total, reach, slope):
    if amount == 2:
        one = jax.random.randint(rng, (), max(1, total - reach), min(reach, total - 1) + 1)
        return jnp.stack([one, total - one])
    tallies = jnp.asarray(profile(amount, total, reach, slope), jnp.int32)
    twos = (amount - 1) // 2
    giver, sink = tallies[1:1 + 2 * twos:2], tallies[2:2 + 2 * twos:2]
    slack = jnp.minimum(giver - 1, reach - sink)
    passed = jax.random.randint(jax.random.fold_in(rng, 1), (twos,), 0, 1 << 20) % (slack + 1)
    tallies = tallies.at[1:1 + 2 * twos:2].set(giver - passed).at[2:2 + 2 * twos:2].set(sink + passed)
    return tallies[jax.random.permutation(jax.random.fold_in(rng, 2), amount)]


def bell_draw(stream_key, extent, width, bound, split=(), held_as=jnp.bfloat16):
    values = jax.random.normal(stream_key, extent, jnp.float32) * width
    if len(split) > 0:
        values = level_of(stream_key, extent, split, -0.22, 0.18) * values
    return jnp.clip(values, min=-bound, max=bound).astype(held_as)


def setup_inputs(seed: int = 0, part: int = 0) -> dict:
    seeds = jax.random.split(jax.random.key(seed), 6)
    part_splits = jax.random.split(jax.random.fold_in(seeds[5], part), 6)
    queries = draw_queries(jax.random.fold_in(jax.random.fold_in(seeds[5], part), 71), part)
    keys = draw_keys(jax.random.fold_in(jax.random.fold_in(seeds[5], part), 71), part)
    values = bell_draw(part_splits[2], (CONTEXT_TOKENS, KEY_VALUE_HEADS * HEAD_SIZE), 1.0, 6.0, ((0, 16), (1, 2)))
    doc_lengths = uneven(part_splits[3], NDOC, CONTEXT_TOKENS, CONTEXT_TOKENS // 2, 2).astype(jnp.int32)
    owner_map = jax.vmap(lambda own: jax.random.permutation(own, N_CTX))(jax.random.split(part_splits[4], N_CTX)).reshape((N_CTX, N_CTX)).astype(jnp.int32)
    return {"queries": queries, "keys": keys, "values": values, "doc_lengths": doc_lengths, "owner_map": owner_map}


MASKED = -1e+30

def doc_index(doc_lengths, positions):
    doc_ends = jnp.cumsum(doc_lengths).astype(jnp.int32)
    return lax.optimization_barrier(jnp.sum((doc_ends[None, :] <= positions[:, None]).astype(jnp.int32), axis=1))

def reference(queries, keys, values, doc_lengths, owner_map):
    query_group_size = QUERY_HEADS // KEY_VALUE_HEADS
    softmax_scale = 1.0 / math.sqrt(HEAD_SIZE)
    token_pos = jnp.arange(CONTEXT_TOKENS, dtype=jnp.int32)
    token_docs = doc_index(doc_lengths, token_pos)
    widened_keys = keys.astype(jnp.float32).reshape(CONTEXT_TOKENS, KEY_VALUE_HEADS, HEAD_SIZE)
    widened_values = values.astype(jnp.float32).reshape(CONTEXT_TOKENS, KEY_VALUE_HEADS, HEAD_SIZE)

    def one_block(block_start):
        block_of_queries = lax.dynamic_slice_in_dim(queries, block_start, TOKENS_PER_SHARD, 0)
        block_of_queries = block_of_queries.astype(jnp.float32).reshape(TOKENS_PER_SHARD, KEY_VALUE_HEADS, query_group_size, HEAD_SIZE)
        query_pos = block_start + jnp.arange(TOKENS_PER_SHARD, dtype=jnp.int32)
        query_docs = doc_index(doc_lengths, query_pos)
        visible = (token_pos[None, :] <= query_pos[:, None]) & (token_docs[None, :] == query_docs[:, None])
        scores = jnp.einsum('qkgd,tkd->kgqt', block_of_queries, widened_keys) * softmax_scale
        scores = jnp.where(visible[None, None], scores, MASKED)
        row_peak = lax.optimization_barrier(jnp.max(scores, axis=-1, keepdims=True))
        weights = jnp.where(visible[None, None], jnp.exp(scores - row_peak), 0.0)
        totals = lax.optimization_barrier(jnp.sum(weights, axis=-1))
        rounded = lax.optimization_barrier(weights.astype(jnp.bfloat16)).astype(jnp.float32)
        mixed = jnp.einsum('kgqt,tkd->kgqd', rounded, widened_values) / totals[..., None]
        return mixed.transpose(2, 0, 1, 3).reshape(TOKENS_PER_SHARD, QUERY_HEADS * HEAD_SIZE).astype(jnp.bfloat16)
    block_starts = jnp.arange(N_CTX, dtype=jnp.int32) * TOKENS_PER_SHARD
    attended = lax.map(one_block, block_starts).reshape(CONTEXT_TOKENS, QUERY_HEADS * HEAD_SIZE)
    slot_ids = jnp.arange(N_CTX, dtype=jnp.int32)
    chosen_block = lax.optimization_barrier(jnp.sum(slot_ids[None, None, :] * (owner_map[None, :, :] == slot_ids[:, None, None]).astype(jnp.int32), axis=2))
    row_order = slot_ids[None, :, None] * TOKENS_PER_SHARD + chosen_block[:, :, None] * BR + jnp.arange(BR, dtype=jnp.int32)[None, None, :]
    return jnp.take(attended, row_order.reshape(-1).astype(jnp.int32), axis=0)
```

```python
import math

import jax
import jax.numpy as jnp
from jax import lax
from jax.experimental import pallas as pl
from jax.experimental.pallas import tpu as pltpu
from jax.sharding import PartitionSpec as P

HEAD = 128
CTX = 16
TOK = 128
BR = 8
NDOC = 16
GROUPS = 4
GROUP_HEADS = 4
PART = 32
REACH = 8
CHUNK = 384
MASKED = -1e30
SCALE = math.log2(math.e) / math.sqrt(HEAD)
ROWS_BY_ROWS = (((1,), (1,)), ((), ()))
ROWS_BY_COLS = (((1,), (0,)), ((), ()))


def dot(a, b, dims):
    return lax.dot_general(a, b, dims, preferred_element_type=jnp.float32)


def pack_kernel(owner_ref, q_ref, k_ref, v_ref, out_ref):
    me = lax.axis_index("ctx")
    lane = lax.broadcasted_iota(jnp.int32, (1, TOK), 1)
    goal = lane % BR
    for b in range(CTX):
        owner = owner_ref[me, b]
        rank = ((owner // 8) * 2 + owner % 2) * 4 + (owner // 2) % 4
        goal = goal + jnp.where(lane // BR == b, rank * BR, 0)
    row = lax.broadcasted_iota(jnp.int32, (TOK, TOK), 0)
    order = jnp.where(row == goal, 1.0, 0.0).astype(jnp.bfloat16)
    moved = dot(order, q_ref[...], ROWS_BY_COLS).astype(jnp.bfloat16)
    for g in range(GROUPS):
        cols = slice(g * HEAD, (g + 1) * HEAD)
        keys = k_ref[:, cols]
        vals = v_ref[:, cols].T
        for part in range(4):
            dest = (part // 2) * 8 + g * 2 + part % 2
            rows = slice(part * PART, (part + 1) * PART)
            for h in range(GROUP_HEADS):
                at = (g * GROUP_HEADS + h) * HEAD
                out_ref[dest, h * PART : (h + 1) * PART, :] = moved[rows, at : at + HEAD]
            out_ref[dest, 128:256, :] = keys
            out_ref[dest, 256:384, :] = vals


def attend_kernel(doc_ref, owner_ref, data_ref, out_ref, acc_ref):
    me = lax.axis_index("ctx")
    lane = lax.broadcasted_iota(jnp.int32, (CTX, TOK), 1)
    shard = lax.broadcasted_iota(jnp.int32, (CTX, TOK), 0)
    owner = (me // 8) * 8 + ((lane // BR) % 4) * 2 + me % 2
    owners = owner_ref[...]
    pos = shard * TOK + lane % BR
    for b in range(CTX):
        pos = pos + jnp.where(owners[:, b : b + 1] == owner, b * BR, 0)
    start = jnp.zeros((CTX, TOK), jnp.int32)
    end = jnp.int32(0)
    for n in range(NDOC - 1):
        end = end + doc_ref[n]
        start = jnp.where(pos >= end, end, start)
    key_at = lax.broadcasted_iota(jnp.int32, (TOK, TOK), 0)

    def scores(pair):
        shards = (2 * pair, 2 * pair + 1)
        tiles = range(max(0, shards[0] - REACH), shards[1] + 1)
        q = jnp.concatenate([data_ref[s, 0:128, :] for s in shards], 0)
        kept = ({}, {})
        peak = [None, None]
        for kb in tiles:
            both = dot(data_ref[kb, 128:256, :], q, ROWS_BY_ROWS)
            for i, s in enumerate(shards):
                if not s - REACH <= kb <= s:
                    continue
                one = both[:, i * TOK : (i + 1) * TOK]
                seen = key_at >= start[s : s + 1] - kb * TOK
                if kb == s:
                    seen = seen & (key_at <= pos[s : s + 1] - kb * TOK)
                one = jnp.where(seen, one, MASKED)
                kept[i][kb] = one
                top = jnp.max(one.reshape(16, 8, TOK), axis=0)
                peak[i] = top if peak[i] is None else jnp.maximum(peak[i], top)
        return shards, tiles, kept, peak

    def finish(state):
        shards, tiles, kept, peak = state
        weights, totals = [], []
        for i in range(2):
            top = jnp.max(peak[i], axis=0, keepdims=True) * SCALE
            total = jnp.zeros((8, TOK), jnp.float32)
            rounded = {}
            for kb, one in kept[i].items():
                w = jnp.exp2(one * SCALE - top)
                total = total + jnp.sum(w.reshape(16, 8, TOK), axis=0)
                rounded[kb] = w.astype(jnp.bfloat16)
            weights.append(rounded)
            totals.append(jnp.sum(total, axis=0, keepdims=True))
        none = jnp.zeros((TOK, TOK), jnp.bfloat16)
        wide = jnp.concatenate(
            [jnp.concatenate([weights[i].get(kb, none) for i in range(2)], 1) for kb in tiles], 0
        )
        vals = jnp.concatenate([data_ref[kb, 256:384, :] for kb in tiles], 1)
        mixed = dot(vals, wide, ROWS_BY_COLS)
        for i, s in enumerate(shards):
            rows = (mixed[:, i * TOK : (i + 1) * TOK] * (1.0 / totals[i])).T
            for h in range(GROUP_HEADS):
                for y in range(4):
                    at = h * PART + y * BR
                    acc_ref[y, s * BR : (s + 1) * BR, h * HEAD : (h + 1) * HEAD] = rows[at : at + BR]

    ahead = scores(0)
    for pair in range(1, CTX // 2):
        following = scores(pair)
        finish(ahead)
        ahead = following
    finish(ahead)
    out_ref[...] = acc_ref[...].astype(jnp.bfloat16)


SMEM = pl.BlockSpec(memory_space=pltpu.SMEM)
VMEM = pl.BlockSpec(memory_space=pltpu.VMEM)


def body(queries, keys, values, doc_lengths, owner_map):
    packed = pl.pallas_call(
        pack_kernel,
        out_shape=jax.ShapeDtypeStruct((CTX, CHUNK, HEAD), jnp.bfloat16),
        in_specs=[SMEM, VMEM, VMEM, VMEM],
        out_specs=VMEM,
        compiler_params=pltpu.CompilerParams(vmem_limit_bytes=24 << 20),
        name="pack",
    )(owner_map, queries, keys, values)
    data = lax.all_to_all(packed, "ctx", 0, 0, tiled=True)
    mixed = pl.pallas_call(
        attend_kernel,
        out_shape=jax.ShapeDtypeStruct((4, TOK, GROUP_HEADS * HEAD), jnp.bfloat16),
        in_specs=[SMEM, VMEM, VMEM],
        out_specs=VMEM,
        scratch_shapes=[pltpu.VMEM((4, TOK, GROUP_HEADS * HEAD), jnp.float32)],
        compiler_params=pltpu.CompilerParams(vmem_limit_bytes=40 << 20),
        name="attend",
    )(doc_lengths, owner_map, data)
    rings = [[x * 8 + y * 2 + c for y in range(4)] for x in range(2) for c in range(2)]
    back = lax.all_to_all(mixed, "ctx", 0, 0, tiled=True, axis_index_groups=rings)
    return back.transpose(1, 0, 2).reshape(TOK, GROUPS * GROUP_HEADS * HEAD)


def solution(mesh):
    placed = (
        P(("dp", "ctx"), "head"),
        P(("dp", "ctx"), "head"),
        P(("dp", "ctx"), "head"),
        P("dp"),
        P("dp", None),
    )
    return jax.shard_map(
        body, mesh=mesh, in_specs=placed, out_specs=P(("dp", "ctx"), "head"), check_vma=False
    )
```

```python
import math

import jax
import jax.numpy as jnp
from jax import lax
from jax.experimental import pallas as pl
from jax.experimental.pallas import tpu as pltpu
from jax.sharding import PartitionSpec as P

HEAD = 128
CTX = 16
TOK = 128
BR = 8
NDOC = 16
GROUPS = 4
GROUP_HEADS = 4
PART = 32
REACH = 8
CHUNK = 256
MASKED = -1e30
SCALE = math.log2(math.e) / math.sqrt(HEAD)
ROWS_BY_ROWS = (((1,), (1,)), ((), ()))
ROWS_BY_COLS = (((1,), (0,)), ((), ()))


def dot(a, b, dims):
    return lax.dot_general(a, b, dims, preferred_element_type=jnp.float32)


def pack_kernel(owner_any, doc_any, q_any, k_any, v_any, out_ref, rows_ref, owner_ref, owners_ref, doc_ref, q_ref, k_ref, v_ref, sems):
    me = lax.axis_index("ctx")
    moves = (
        (owner_any, owner_ref),
        (owner_any, owners_ref),
        (doc_any, doc_ref),
        (k_any, k_ref),
        (v_any, v_ref),
        (q_any, q_ref),
    )
    copies = [pltpu.make_async_copy(src, dst, sems.at[i]) for i, (src, dst) in enumerate(moves)]
    for copy in copies:
        copy.start()
    for copy in copies[:3]:
        copy.wait()
    one_lane = lax.broadcasted_iota(jnp.int32, (1, TOK), 1)
    goal = one_lane % BR
    for b in range(CTX):
        owner = owner_ref[me, b]
        rank = ((owner // 8) * 2 + owner % 2) * 4 + (owner // 2) % 4
        goal = goal + jnp.where(one_lane // BR == b, rank * BR, 0)
    row = lax.broadcasted_iota(jnp.int32, (TOK, TOK), 0)
    order = jnp.where(row == goal, 1.0, 0.0).astype(jnp.bfloat16)

    lane = lax.broadcasted_iota(jnp.int32, (CTX, TOK), 1)
    shard = lax.broadcasted_iota(jnp.int32, (CTX, TOK), 0)
    mine = (me // 8) * 8 + ((lane // BR) % 4) * 2 + me % 2
    owners = owners_ref[...]
    pos = shard * TOK + lane % BR
    for b in range(CTX):
        pos = pos + jnp.where(owners[:, b : b + 1] == mine, b * BR, 0)
    start = jnp.zeros((CTX, TOK), jnp.int32)
    end = jnp.int32(0)
    for n in range(NDOC - 1):
        end = end + doc_ref[n]
        start = jnp.where(pos >= end, end, start)
    rows_ref[0] = pos
    rows_ref[1] = start

    for copy in copies[3:5]:
        copy.wait()
    for g in range(GROUPS):
        cols = slice(g * HEAD, (g + 1) * HEAD)
        keys = k_ref[:, cols]
        vals = v_ref[:, cols].T
        for part in range(4):
            dest = (part // 2) * 8 + g * 2 + part % 2
            out_ref[dest, 128:256, :] = vals if part % 2 else keys
    copies[5].wait()
    for g in range(GROUPS):
        wide = slice(g * GROUP_HEADS * HEAD, (g + 1) * GROUP_HEADS * HEAD)
        moved = dot(order, q_ref[:, wide], ROWS_BY_COLS).astype(jnp.bfloat16)
        for part in range(4):
            dest = (part // 2) * 8 + g * 2 + part % 2
            for h in range(GROUP_HEADS):
                out_ref[dest, h * PART : (h + 1) * PART, :] = moved[
                    part * PART : (part + 1) * PART, h * HEAD : (h + 1) * HEAD
                ]


def attend_kernel(rows_ref, data_ref, both_ref, out_ref, acc_ref):
    key_at = lax.broadcasted_iota(jnp.int32, (TOK, TOK), 0)

    def scores(pair):
        shards = (2 * pair, 2 * pair + 1)
        tiles = range(max(0, shards[0] - REACH), shards[1] + 1)
        q = jnp.concatenate([data_ref[s, 0:128, :] for s in shards], 0)
        kept = ({}, {})
        peak = [None, None]
        for kb in tiles:
            both = dot(both_ref[0, kb], q, ROWS_BY_ROWS)
            for i, s in enumerate(shards):
                if not s - REACH <= kb <= s:
                    continue
                one = both[:, i * TOK : (i + 1) * TOK]
                seen = key_at >= rows_ref[1, s : s + 1, :] - kb * TOK
                if kb == s:
                    seen = seen & (key_at <= rows_ref[0, s : s + 1, :] - kb * TOK)
                one = jnp.where(seen, one, MASKED)
                kept[i][kb] = one
                top = jnp.max(one.reshape(16, 8, TOK), axis=0)
                peak[i] = top if peak[i] is None else jnp.maximum(peak[i], top)
        return shards, tiles, kept, peak

    def finish(state):
        shards, tiles, kept, peak = state
        weights, totals = [], []
        for i in range(2):
            top = jnp.max(peak[i], axis=0, keepdims=True) * SCALE
            total = jnp.zeros((8, TOK), jnp.float32)
            rounded = {}
            for kb, one in kept[i].items():
                w = jnp.exp2(one * SCALE - top)
                total = total + jnp.sum(w.reshape(16, 8, TOK), axis=0)
                rounded[kb] = w.astype(jnp.bfloat16)
            weights.append(rounded)
            totals.append(jnp.sum(total, axis=0, keepdims=True))
        none = jnp.zeros((TOK, TOK), jnp.bfloat16)
        wide = jnp.concatenate(
            [jnp.concatenate([weights[i].get(kb, none) for i in range(2)], 1) for kb in tiles], 0
        )
        vals = jnp.concatenate([both_ref[1, kb] for kb in tiles], 1)
        mixed = dot(vals, wide, ROWS_BY_COLS)
        for i, s in enumerate(shards):
            rows = (mixed[:, i * TOK : (i + 1) * TOK] * (1.0 / totals[i])).T
            for h in range(GROUP_HEADS):
                for y in range(4):
                    at = h * PART + y * BR
                    acc_ref[y, s * BR : (s + 1) * BR, h * HEAD : (h + 1) * HEAD] = rows[at : at + BR]

    ahead = scores(0)
    for pair in range(1, CTX // 2):
        following = scores(pair)
        finish(ahead)
        ahead = following
    finish(ahead)
    out_ref[...] = acc_ref[...].astype(jnp.bfloat16)


def unpack_kernel(in_ref, out_any, sems):
    wide = GROUP_HEADS * HEAD
    copies = [
        pltpu.make_async_copy(in_ref.at[g], out_any.at[:, g * wide : (g + 1) * wide], sems.at[g])
        for g in range(GROUPS)
    ]
    for copy in copies:
        copy.start()
    for copy in copies:
        copy.wait()


VMEM = pl.BlockSpec(memory_space=pltpu.VMEM)
ANY = pl.BlockSpec(memory_space=pl.ANY)


def body(queries, keys, values, doc_lengths, owner_map):
    packed, rows = pl.pallas_call(
        pack_kernel,
        out_shape=(
            jax.ShapeDtypeStruct((CTX, CHUNK, HEAD), jnp.bfloat16),
            jax.ShapeDtypeStruct((2, CTX, TOK), jnp.int32),
        ),
        in_specs=[ANY] * 5,
        out_specs=(VMEM, VMEM),
        scratch_shapes=[
            pltpu.SMEM((CTX, CTX), jnp.int32),
            pltpu.VMEM((CTX, CTX), jnp.int32),
            pltpu.SMEM((NDOC,), jnp.int32),
            pltpu.VMEM(queries.shape, jnp.bfloat16),
            pltpu.VMEM(keys.shape, jnp.bfloat16),
            pltpu.VMEM(values.shape, jnp.bfloat16),
            pltpu.SemaphoreType.DMA((6,)),
        ],
        compiler_params=pltpu.CompilerParams(vmem_limit_bytes=60 << 20),
        name="pack",
    )(owner_map, doc_lengths, queries, keys, values)
    data = lax.all_to_all(packed, "ctx", 0, 0, tiled=True)
    chips = [[2 * i, 2 * i + 1] for i in range(CTX // 2)]
    both = lax.all_gather(data[:, TOK:], "ctx", axis=0, axis_index_groups=chips)
    mixed = pl.pallas_call(
        attend_kernel,
        out_shape=jax.ShapeDtypeStruct((4, TOK, GROUP_HEADS * HEAD), jnp.bfloat16),
        in_specs=[VMEM, VMEM, VMEM],
        out_specs=VMEM,
        scratch_shapes=[pltpu.VMEM((4, TOK, GROUP_HEADS * HEAD), jnp.float32)],
        compiler_params=pltpu.CompilerParams(vmem_limit_bytes=40 << 20),
        name="attend",
    )(rows, data, both)
    rings = [[x * 8 + y * 2 + c for y in range(4)] for x in range(2) for c in range(2)]
    back = lax.all_to_all(mixed, "ctx", 0, 0, tiled=True, axis_index_groups=rings)
    return pl.pallas_call(
        unpack_kernel,
        out_shape=jax.ShapeDtypeStruct(queries.shape, jnp.bfloat16),
        in_specs=[VMEM],
        out_specs=ANY,
        scratch_shapes=[pltpu.SemaphoreType.DMA((GROUPS,))],
        compiler_params=pltpu.CompilerParams(vmem_limit_bytes=16 << 20),
        name="unpack",
    )(back)


def solution(mesh):
    placed = (
        P(("dp", "ctx"), "head"),
        P(("dp", "ctx"), "head"),
        P(("dp", "ctx"), "head"),
        P("dp"),
        P("dp", None),
    )
    return jax.shard_map(
        body, mesh=mesh, in_specs=placed, out_specs=P(("dp", "ctx"), "head"), check_vma=False
    )
```

```python
import math

import jax
import jax.numpy as jnp
from jax import lax
from jax.experimental import pallas as pl
from jax.experimental.pallas import tpu as pltpu
from jax.sharding import PartitionSpec as P

HEAD = 128
CTX = 16
TOK = 128
BR = 8
NDOC = 16
GROUPS = 4
GROUP_HEADS = 4
PART = 32
REACH = 8
CHUNK = 256
MASKED = -1e30
SCALE = math.log2(math.e) / math.sqrt(HEAD)
ROWS_BY_ROWS = (((1,), (1,)), ((), ()))
ROWS_BY_COLS = (((1,), (0,)), ((), ()))


def dot(a, b, dims):
    return lax.dot_general(a, b, dims, preferred_element_type=jnp.float32)


def pack_kernel(owner_any, doc_any, q_any, k_any, v_any, out_ref, rows_ref, owner_ref, owners_ref, doc_ref, q_ref, k_ref, v_ref, sems):
    me = lax.axis_index("ctx")
    moves = (
        (owner_any, owner_ref),
        (owner_any, owners_ref),
        (doc_any, doc_ref),
        (k_any, k_ref),
        (v_any, v_ref),
        (q_any, q_ref),
    )
    copies = [pltpu.make_async_copy(src, dst, sems.at[i]) for i, (src, dst) in enumerate(moves)]
    for copy in copies:
        copy.start()
    for copy in copies[:3]:
        copy.wait()
    one_lane = lax.broadcasted_iota(jnp.int32, (1, TOK), 1)
    goal = one_lane % BR
    for b in range(CTX):
        owner = owner_ref[me, b]
        rank = ((owner // 8) * 2 + owner % 2) * 4 + (owner // 2) % 4
        goal = goal + jnp.where(one_lane // BR == b, rank * BR, 0)
    row = lax.broadcasted_iota(jnp.int32, (TOK, TOK), 0)
    order = jnp.where(row == goal, 1.0, 0.0).astype(jnp.bfloat16)

    lane = lax.broadcasted_iota(jnp.int32, (CTX, TOK), 1)
    shard = lax.broadcasted_iota(jnp.int32, (CTX, TOK), 0)
    mine = (me // 8) * 8 + ((lane // BR) % 4) * 2 + me % 2
    owners = owners_ref[...]
    pos = shard * TOK + lane % BR
    for b in range(CTX):
        pos = pos + jnp.where(owners[:, b : b + 1] == mine, b * BR, 0)
    start = jnp.zeros((CTX, TOK), jnp.int32)
    end = jnp.int32(0)
    for n in range(NDOC - 1):
        end = end + doc_ref[n]
        start = jnp.where(pos >= end, end, start)
    rows_ref[0] = pos
    rows_ref[1] = start

    for copy in copies[3:5]:
        copy.wait()
    for g in range(GROUPS):
        cols = slice(g * HEAD, (g + 1) * HEAD)
        keys = k_ref[:, cols]
        vals = v_ref[:, cols].T
        for part in range(4):
            dest = (part // 2) * 8 + g * 2 + part % 2
            out_ref[dest, 128:256, :] = vals if part % 2 else keys
    copies[5].wait()
    for g in range(GROUPS):
        wide = slice(g * GROUP_HEADS * HEAD, (g + 1) * GROUP_HEADS * HEAD)
        moved = dot(order, q_ref[:, wide], ROWS_BY_COLS).astype(jnp.bfloat16)
        for part in range(4):
            dest = (part // 2) * 8 + g * 2 + part % 2
            for h in range(GROUP_HEADS):
                out_ref[dest, h * PART : (h + 1) * PART, :] = moved[
                    part * PART : (part + 1) * PART, h * HEAD : (h + 1) * HEAD
                ]


def attend_kernel(rows_ref, data_ref, other_ref, out_ref, acc_ref, both_ref):
    first = lax.axis_index("ctx") % 2 == 0
    for s in range(CTX):
        own, far = data_ref[s, TOK:, :], other_ref[s]
        both_ref[0, s] = jnp.where(first, own, far)
        both_ref[1, s] = jnp.where(first, far, own)
    key_at = lax.broadcasted_iota(jnp.int32, (TOK, TOK), 0)

    def scores(pair):
        shards = (2 * pair, 2 * pair + 1)
        tiles = range(max(0, shards[0] - REACH), shards[1] + 1)
        q = jnp.concatenate([data_ref[s, 0:128, :] for s in shards], 0)
        kept = ({}, {})
        peak = [None, None]
        for kb in tiles:
            both = dot(both_ref[0, kb], q, ROWS_BY_ROWS)
            for i, s in enumerate(shards):
                if not s - REACH <= kb <= s:
                    continue
                one = both[:, i * TOK : (i + 1) * TOK]
                seen = key_at >= rows_ref[1, s : s + 1, :] - kb * TOK
                if kb == s:
                    seen = seen & (key_at <= rows_ref[0, s : s + 1, :] - kb * TOK)
                one = jnp.where(seen, one, MASKED)
                kept[i][kb] = one
                top = jnp.max(one.reshape(16, 8, TOK), axis=0)
                peak[i] = top if peak[i] is None else jnp.maximum(peak[i], top)
        return shards, tiles, kept, peak

    def finish(state):
        shards, tiles, kept, peak = state
        weights, totals = [], []
        for i in range(2):
            top = jnp.max(peak[i], axis=0, keepdims=True) * SCALE
            total = jnp.zeros((8, TOK), jnp.float32)
            rounded = {}
            for kb, one in kept[i].items():
                w = jnp.exp2(one * SCALE - top)
                total = total + jnp.sum(w.reshape(16, 8, TOK), axis=0)
                rounded[kb] = w.astype(jnp.bfloat16)
            weights.append(rounded)
            totals.append(jnp.sum(total, axis=0, keepdims=True))
        none = jnp.zeros((TOK, TOK), jnp.bfloat16)
        wide = jnp.concatenate(
            [jnp.concatenate([weights[i].get(kb, none) for i in range(2)], 1) for kb in tiles], 0
        )
        vals = jnp.concatenate([both_ref[1, kb] for kb in tiles], 1)
        mixed = dot(vals, wide, ROWS_BY_COLS)
        for i, s in enumerate(shards):
            rows = (mixed[:, i * TOK : (i + 1) * TOK] * (1.0 / totals[i])).T
            for h in range(GROUP_HEADS):
                for y in range(4):
                    at = h * PART + y * BR
                    acc_ref[y, s * BR : (s + 1) * BR, h * HEAD : (h + 1) * HEAD] = rows[at : at + BR]

    ahead = scores(0)
    for pair in range(1, CTX // 2):
        following = scores(pair)
        finish(ahead)
        ahead = following
    finish(ahead)
    out_ref[...] = acc_ref[...].astype(jnp.bfloat16)


def unpack_kernel(in_ref, out_any, sems):
    wide = GROUP_HEADS * HEAD
    copies = [
        pltpu.make_async_copy(in_ref.at[g], out_any.at[:, g * wide : (g + 1) * wide], sems.at[g])
        for g in range(GROUPS)
    ]
    for copy in copies:
        copy.start()
    for copy in copies:
        copy.wait()


VMEM = pl.BlockSpec(memory_space=pltpu.VMEM)
ANY = pl.BlockSpec(memory_space=pl.ANY)


def body(queries, keys, values, doc_lengths, owner_map):
    packed, rows = pl.pallas_call(
        pack_kernel,
        out_shape=(
            jax.ShapeDtypeStruct((CTX, CHUNK, HEAD), jnp.bfloat16),
            jax.ShapeDtypeStruct((2, CTX, TOK), jnp.int32),
        ),
        in_specs=[ANY] * 5,
        out_specs=(VMEM, VMEM),
        scratch_shapes=[
            pltpu.SMEM((CTX, CTX), jnp.int32),
            pltpu.VMEM((CTX, CTX), jnp.int32),
            pltpu.SMEM((NDOC,), jnp.int32),
            pltpu.VMEM(queries.shape, jnp.bfloat16),
            pltpu.VMEM(keys.shape, jnp.bfloat16),
            pltpu.VMEM(values.shape, jnp.bfloat16),
            pltpu.SemaphoreType.DMA((6,)),
        ],
        compiler_params=pltpu.CompilerParams(vmem_limit_bytes=60 << 20),
        name="pack",
    )(owner_map, doc_lengths, queries, keys, values)
    data = lax.all_to_all(packed, "ctx", 0, 0, tiled=True)
    other = lax.ppermute(data[:, TOK:], "ctx", [(i, i ^ 1) for i in range(CTX)])
    mixed = pl.pallas_call(
        attend_kernel,
        out_shape=jax.ShapeDtypeStruct((4, TOK, GROUP_HEADS * HEAD), jnp.bfloat16),
        in_specs=[VMEM, VMEM, VMEM],
        out_specs=VMEM,
        scratch_shapes=[
            pltpu.VMEM((4, TOK, GROUP_HEADS * HEAD), jnp.float32),
            pltpu.VMEM((2, CTX, TOK, HEAD), jnp.bfloat16),
        ],
        compiler_params=pltpu.CompilerParams(vmem_limit_bytes=40 << 20),
        name="attend",
    )(rows, data, other)
    rings = [[x * 8 + y * 2 + c for y in range(4)] for x in range(2) for c in range(2)]
    back = lax.all_to_all(mixed, "ctx", 0, 0, tiled=True, axis_index_groups=rings)
    return pl.pallas_call(
        unpack_kernel,
        out_shape=jax.ShapeDtypeStruct(queries.shape, jnp.bfloat16),
        in_specs=[VMEM],
        out_specs=ANY,
        scratch_shapes=[pltpu.SemaphoreType.DMA((GROUPS,))],
        compiler_params=pltpu.CompilerParams(vmem_limit_bytes=16 << 20),
        name="unpack",
    )(back)


def solution(mesh):
    placed = (
        P(("dp", "ctx"), "head"),
        P(("dp", "ctx"), "head"),
        P(("dp", "ctx"), "head"),
        P("dp"),
        P("dp", None),
    )
    return jax.shard_map(
        body, mesh=mesh, in_specs=placed, out_specs=P(("dp", "ctx"), "head"), check_vma=False
    )
```

```python
import math

import jax
import jax.numpy as jnp
from jax import lax
from jax.experimental import pallas as pl
from jax.experimental.pallas import tpu as pltpu
from jax.sharding import PartitionSpec as P

HEAD = 128
CTX = 16
TOK = 128
BR = 8
NDOC = 16
GROUPS = 4
GROUP_HEADS = 4
PART = 32
REACH = 8
CHUNK = 256
MASKED = -1e30
SCALE = math.log2(math.e) / math.sqrt(HEAD)
ROWS_BY_ROWS = (((1,), (1,)), ((), ()))
ROWS_BY_COLS = (((1,), (0,)), ((), ()))


def dot(a, b, dims):
    return lax.dot_general(a, b, dims, preferred_element_type=jnp.float32)


def pack_kernel(owner_any, doc_any, q_any, k_any, v_any, out_ref, rows_ref, owner_ref, owners_ref, doc_ref, q_ref, k_ref, v_ref, sems):
    me = lax.axis_index("ctx")
    moves = (
        (owner_any, owner_ref),
        (owner_any, owners_ref),
        (doc_any, doc_ref),
        (k_any, k_ref),
        (v_any, v_ref),
        (q_any, q_ref),
    )
    copies = [pltpu.make_async_copy(src, dst, sems.at[i]) for i, (src, dst) in enumerate(moves)]
    for copy in copies:
        copy.start()
    for copy in copies[:3]:
        copy.wait()
    one_lane = lax.broadcasted_iota(jnp.int32, (1, TOK), 1)
    goal = one_lane % BR
    for b in range(CTX):
        owner = owner_ref[me, b]
        rank = ((owner // 8) * 2 + owner % 2) * 4 + (owner // 2) % 4
        goal = goal + jnp.where(one_lane // BR == b, rank * BR, 0)
    row = lax.broadcasted_iota(jnp.int32, (TOK, TOK), 0)
    order = jnp.where(row == goal, 1.0, 0.0).astype(jnp.bfloat16)

    lane = lax.broadcasted_iota(jnp.int32, (CTX, TOK), 1)
    shard = lax.broadcasted_iota(jnp.int32, (CTX, TOK), 0)
    mine = (me // 8) * 8 + ((lane // BR) % 4) * 2 + me % 2
    owners = owners_ref[...]
    pos = shard * TOK + lane % BR
    for b in range(CTX):
        pos = pos + jnp.where(owners[:, b : b + 1] == mine, b * BR, 0)
    start = jnp.zeros((CTX, TOK), jnp.int32)
    end = jnp.int32(0)
    for n in range(NDOC - 1):
        end = end + doc_ref[n]
        start = jnp.where(pos >= end, end, start)
    rows_ref[0] = pos
    rows_ref[1] = start

    for copy in copies[3:5]:
        copy.wait()
    for g in range(GROUPS):
        cols = slice(g * HEAD, (g + 1) * HEAD)
        keys = k_ref[:, cols]
        vals = v_ref[:, cols]
        for part in range(4):
            dest = (part // 2) * 8 + g * 2 + part % 2
            half = slice(part % 2 * 64, part % 2 * 64 + 64)
            out_ref[dest, 128:192, :] = keys[half]
            out_ref[dest, 192:256, :] = vals[half]
    copies[5].wait()
    for g in range(GROUPS):
        wide = slice(g * GROUP_HEADS * HEAD, (g + 1) * GROUP_HEADS * HEAD)
        moved = dot(order, q_ref[:, wide], ROWS_BY_COLS).astype(jnp.bfloat16)
        for part in range(4):
            dest = (part // 2) * 8 + g * 2 + part % 2
            for h in range(GROUP_HEADS):
                out_ref[dest, h * PART : (h + 1) * PART, :] = moved[
                    part * PART : (part + 1) * PART, h * HEAD : (h + 1) * HEAD
                ]


def attend_half(second, rows_ref, data_ref, half_ref, offset, sums_ref, peaks_ref, totals_ref, emit):
    half = (lax.axis_index("ctx") + second) % 2
    row = lax.broadcasted_iota(jnp.int32, (TOK, TOK), 0)
    key_at = (row // 64) * TOK + row % 64 + half * 64

    def keys(m):
        return half_ref[2 * m : 2 * m + 2, offset : offset + 64, :].reshape(TOK, HEAD)

    def values(m):
        return half_ref[2 * m : 2 * m + 2, offset + 64 : offset + 128, :].reshape(TOK, HEAD).T

    turned = [values(m) for m in range(CTX // 2)]

    def scores(pair):
        tiles = range(max(0, pair - REACH // 2), pair + 1)
        q = data_ref[2 * pair : 2 * pair + 2, 0:128, :].reshape(2 * TOK, HEAD)
        kept = []
        peak = [None, None]
        for m in tiles:
            both = dot(keys(m), q, ROWS_BY_ROWS)
            ones = []
            for i in range(2):
                s = 2 * pair + i
                one = both[:, i * TOK : (i + 1) * TOK]
                seen = key_at >= rows_ref[1, s : s + 1, :] - m * 2 * TOK
                if m == pair:
                    seen = seen & (key_at <= rows_ref[0, s : s + 1, :] - m * 2 * TOK)
                one = jnp.where(seen, one, MASKED)
                ones.append(one)
                top = jnp.max(one.reshape(16, 8, TOK), axis=0)
                peak[i] = top if peak[i] is None else jnp.maximum(peak[i], top)
            kept.append(ones)
        return pair, tiles, kept, peak

    def finish(state):
        pair, tiles, kept, peak = state
        tops, totals = [], []
        for i in range(2):
            top = jnp.max(peak[i], axis=0, keepdims=True) * SCALE
            if second:
                top = jnp.maximum(top, peaks_ref[2 * pair + i : 2 * pair + i + 1, :])
            tops.append(top)
            totals.append(jnp.zeros((8, TOK), jnp.float32))
        wide = []
        for ones in kept:
            parts = []
            for i in range(2):
                w = jnp.exp2(ones[i] * SCALE - tops[i])
                totals[i] = totals[i] + jnp.sum(w.reshape(16, 8, TOK), axis=0)
                parts.append(w.astype(jnp.bfloat16))
            wide.append(jnp.concatenate(parts, 1))
        mixed = dot(
            jnp.concatenate([turned[m] for m in tiles], 1), jnp.concatenate(wide, 0), ROWS_BY_COLS
        )
        for i in range(2):
            total = jnp.sum(totals[i], axis=0, keepdims=True)
            emit(2 * pair + i, mixed[:, i * TOK : (i + 1) * TOK], tops[i], total)

    ahead = scores(0)
    for pair in range(1, CTX // 2):
        following = scores(pair)
        finish(ahead)
        ahead = following
    finish(ahead)


def own_kernel(rows_ref, data_ref, sums_ref, peaks_ref, totals_ref):
    def emit(s, mixed, top, total):
        sums_ref[s] = mixed
        peaks_ref[s : s + 1, :] = top
        totals_ref[s : s + 1, :] = total

    attend_half(0, rows_ref, data_ref, data_ref, TOK, None, None, None, emit)


def other_kernel(rows_ref, data_ref, other_ref, sums_ref, peaks_ref, totals_ref, out_ref, acc_ref):
    def emit(s, mixed, top, total):
        shrink = jnp.exp2(peaks_ref[s : s + 1, :] - top)
        total = total + totals_ref[s : s + 1, :] * shrink
        rows = ((mixed + sums_ref[s] * shrink) * (1.0 / total)).T
        for h in range(GROUP_HEADS):
            for y in range(4):
                at = h * PART + y * BR
                acc_ref[y, s * BR : (s + 1) * BR, h * HEAD : (h + 1) * HEAD] = rows[at : at + BR]

    attend_half(1, rows_ref, data_ref, other_ref, 0, sums_ref, peaks_ref, totals_ref, emit)
    out_ref[...] = acc_ref[...].astype(jnp.bfloat16)


def unpack_kernel(in_ref, out_any, sems):
    wide = GROUP_HEADS * HEAD
    copies = [
        pltpu.make_async_copy(in_ref.at[g], out_any.at[:, g * wide : (g + 1) * wide], sems.at[g])
        for g in range(GROUPS)
    ]
    for copy in copies:
        copy.start()
    for copy in copies:
        copy.wait()


VMEM = pl.BlockSpec(memory_space=pltpu.VMEM)
ANY = pl.BlockSpec(memory_space=pl.ANY)


def body(queries, keys, values, doc_lengths, owner_map):
    packed, rows = pl.pallas_call(
        pack_kernel,
        out_shape=(
            jax.ShapeDtypeStruct((CTX, CHUNK, HEAD), jnp.bfloat16),
            jax.ShapeDtypeStruct((2, CTX, TOK), jnp.int32),
        ),
        in_specs=[ANY] * 5,
        out_specs=(VMEM, VMEM),
        scratch_shapes=[
            pltpu.SMEM((CTX, CTX), jnp.int32),
            pltpu.VMEM((CTX, CTX), jnp.int32),
            pltpu.SMEM((NDOC,), jnp.int32),
            pltpu.VMEM(queries.shape, jnp.bfloat16),
            pltpu.VMEM(keys.shape, jnp.bfloat16),
            pltpu.VMEM(values.shape, jnp.bfloat16),
            pltpu.SemaphoreType.DMA((6,)),
        ],
        compiler_params=pltpu.CompilerParams(vmem_limit_bytes=60 << 20),
        name="pack",
    )(owner_map, doc_lengths, queries, keys, values)
    data = lax.all_to_all(packed, "ctx", 0, 0, tiled=True)
    other = lax.ppermute(data[:, TOK:], "ctx", [(i, i ^ 1) for i in range(CTX)])
    sums, peaks, totals = pl.pallas_call(
        own_kernel,
        out_shape=(
            jax.ShapeDtypeStruct((CTX, HEAD, TOK), jnp.float32),
            jax.ShapeDtypeStruct((CTX, TOK), jnp.float32),
            jax.ShapeDtypeStruct((CTX, TOK), jnp.float32),
        ),
        in_specs=[VMEM] * 2,
        out_specs=(VMEM,) * 3,
        compiler_params=pltpu.CompilerParams(vmem_limit_bytes=40 << 20),
        cost_estimate=pl.CostEstimate(flops=10**9, bytes_accessed=3 << 20, transcendentals=10**6),
        name="own_half",
    )(rows, data)
    mixed = pl.pallas_call(
        other_kernel,
        out_shape=jax.ShapeDtypeStruct((4, TOK, GROUP_HEADS * HEAD), jnp.bfloat16),
        in_specs=[VMEM] * 6,
        out_specs=VMEM,
        scratch_shapes=[pltpu.VMEM((4, TOK, GROUP_HEADS * HEAD), jnp.float32)],
        compiler_params=pltpu.CompilerParams(vmem_limit_bytes=40 << 20),
        name="other_half",
    )(rows, data, other, sums, peaks, totals)
    rings = [[x * 8 + y * 2 + c for y in range(4)] for x in range(2) for c in range(2)]
    back = lax.all_to_all(mixed, "ctx", 0, 0, tiled=True, axis_index_groups=rings)
    return pl.pallas_call(
        unpack_kernel,
        out_shape=jax.ShapeDtypeStruct(queries.shape, jnp.bfloat16),
        in_specs=[VMEM],
        out_specs=ANY,
        scratch_shapes=[pltpu.SemaphoreType.DMA((GROUPS,))],
        compiler_params=pltpu.CompilerParams(vmem_limit_bytes=16 << 20),
        name="unpack",
    )(back)


def solution(mesh):
    placed = (
        P(("dp", "ctx"), "head"),
        P(("dp", "ctx"), "head"),
        P(("dp", "ctx"), "head"),
        P("dp"),
        P("dp", None),
    )
    return jax.shard_map(
        body, mesh=mesh, in_specs=placed, out_specs=P(("dp", "ctx"), "head"), check_vma=False
    )
```

```python
import math

import jax
import jax.numpy as jnp
from jax import lax
from jax.experimental import pallas as pl
from jax.experimental.pallas import tpu as pltpu
from jax.sharding import PartitionSpec as P

HEAD = 128
CTX = 16
TOK = 128
BR = 8
NDOC = 16
GROUPS = 4
GROUP_HEADS = 4
PART = 32
REACH = 8
CHUNK = 256
MASKED = -1e30
SCALE = math.log2(math.e) / math.sqrt(HEAD)
ROWS_BY_ROWS = (((1,), (1,)), ((), ()))
ROWS_BY_COLS = (((1,), (0,)), ((), ()))


def dot(a, b, dims):
    return lax.dot_general(a, b, dims, preferred_element_type=jnp.float32)


def pack_kernel(owner_any, doc_any, q_any, k_any, v_any, out_ref, rows_ref, owner_ref, owners_ref, doc_ref, q_ref, k_ref, v_ref, sems):
    me = lax.axis_index("ctx")
    moves = (
        (owner_any, owner_ref),
        (owner_any, owners_ref),
        (doc_any, doc_ref),
        (k_any, k_ref),
        (v_any, v_ref),
        (q_any, q_ref),
    )
    copies = [pltpu.make_async_copy(src, dst, sems.at[i]) for i, (src, dst) in enumerate(moves)]
    for copy in copies:
        copy.start()
    for copy in copies[:3]:
        copy.wait()
    one_lane = lax.broadcasted_iota(jnp.int32, (1, TOK), 1)
    goal = one_lane % BR
    for b in range(CTX):
        owner = owner_ref[me, b]
        rank = ((owner // 8) * 2 + owner % 2) * 4 + (owner // 2) % 4
        goal = goal + jnp.where(one_lane // BR == b, rank * BR, 0)
    row = lax.broadcasted_iota(jnp.int32, (TOK, TOK), 0)
    order = jnp.where(row == goal, 1.0, 0.0).astype(jnp.bfloat16)

    lane = lax.broadcasted_iota(jnp.int32, (CTX, TOK), 1)
    shard = lax.broadcasted_iota(jnp.int32, (CTX, TOK), 0)
    mine = (me // 8) * 8 + ((lane // BR) % 4) * 2 + me % 2
    owners = owners_ref[...]
    pos = shard * TOK + lane % BR
    for b in range(CTX):
        pos = pos + jnp.where(owners[:, b : b + 1] == mine, b * BR, 0)
    start = jnp.zeros((CTX, TOK), jnp.int32)
    end = jnp.int32(0)
    for n in range(NDOC - 1):
        end = end + doc_ref[n]
        start = jnp.where(pos >= end, end, start)
    rows_ref[0] = pos
    rows_ref[1] = start

    for copy in copies[3:5]:
        copy.wait()
    for g in range(GROUPS):
        cols = slice(g * HEAD, (g + 1) * HEAD)
        keys = k_ref[:, cols]
        vals = v_ref[:, cols]
        for part in range(4):
            dest = (part // 2) * 8 + g * 2 + part % 2
            half = slice(part % 2 * 64, part % 2 * 64 + 64)
            out_ref[dest, 128:192, :] = keys[half]
            out_ref[dest, 192:256, :] = vals[half]
    copies[5].wait()
    for g in range(GROUPS):
        wide = slice(g * GROUP_HEADS * HEAD, (g + 1) * GROUP_HEADS * HEAD)
        moved = dot(order, q_ref[:, wide], ROWS_BY_COLS).astype(jnp.bfloat16)
        for part in range(4):
            dest = (part // 2) * 8 + g * 2 + part % 2
            for h in range(GROUP_HEADS):
                out_ref[dest, h * PART : (h + 1) * PART, :] = moved[
                    part * PART : (part + 1) * PART, h * HEAD : (h + 1) * HEAD
                ]


def attend_half(second, rows_ref, data_ref, half_ref, offset, sums_ref, peaks_ref, totals_ref, emit):
    half = (lax.axis_index("ctx") + second) % 2
    row = lax.broadcasted_iota(jnp.int32, (TOK, TOK), 0)
    key_at = (row // 64) * TOK + row % 64 + half * 64

    def keys(m):
        return half_ref[2 * m : 2 * m + 2, offset : offset + 64, :].reshape(TOK, HEAD)

    def values(m):
        return half_ref[2 * m : 2 * m + 2, offset + 64 : offset + 128, :].reshape(TOK, HEAD).T

    turned = [values(m) for m in range(CTX // 2)]

    def scores(pair):
        tiles = range(max(0, pair - REACH // 2), pair + 1)
        q = data_ref[2 * pair : 2 * pair + 2, 0:128, :].reshape(2 * TOK, HEAD)
        kept = []
        peak = [None, None]
        for m in tiles:
            both = dot(keys(m), q, ROWS_BY_ROWS)
            ones = []
            for i in range(2):
                s = 2 * pair + i
                one = both[:, i * TOK : (i + 1) * TOK]
                seen = key_at >= rows_ref[1, s : s + 1, :] - m * 2 * TOK
                if m == pair:
                    seen = seen & (key_at <= rows_ref[0, s : s + 1, :] - m * 2 * TOK)
                one = jnp.where(seen, one, MASKED)
                ones.append(one)
                top = jnp.max(one.reshape(16, 8, TOK), axis=0)
                peak[i] = top if peak[i] is None else jnp.maximum(peak[i], top)
            kept.append(ones)
        return pair, tiles, kept, peak

    def finish(state):
        pair, tiles, kept, peak = state
        tops, totals = [], []
        for i in range(2):
            top = jnp.max(peak[i], axis=0, keepdims=True) * SCALE
            if second:
                top = jnp.maximum(top, peaks_ref[2 * pair + i : 2 * pair + i + 1, :])
            tops.append(top)
            totals.append(jnp.zeros((8, TOK), jnp.float32))
        wide = []
        for ones in kept:
            parts = []
            for i in range(2):
                w = jnp.exp2(ones[i] * SCALE - tops[i])
                totals[i] = totals[i] + jnp.sum(w.reshape(16, 8, TOK), axis=0)
                parts.append(w.astype(jnp.bfloat16))
            wide.append(jnp.concatenate(parts, 1))
        mixed = dot(
            jnp.concatenate([turned[m] for m in tiles], 1), jnp.concatenate(wide, 0), ROWS_BY_COLS
        )
        for i in range(2):
            total = jnp.sum(totals[i], axis=0, keepdims=True)
            emit(2 * pair + i, mixed[:, i * TOK : (i + 1) * TOK], tops[i], total)

    ahead = scores(0)
    for pair in range(1, CTX // 2):
        following = scores(pair)
        finish(ahead)
        ahead = following
    finish(ahead)


def own_kernel(rows_ref, data_ref, sums_ref, peaks_ref, totals_ref):
    def emit(s, mixed, top, total):
        sums_ref[s] = mixed
        peaks_ref[s : s + 1, :] = top
        totals_ref[s : s + 1, :] = total

    attend_half(0, rows_ref, data_ref, data_ref, TOK, None, None, None, emit)


def other_kernel(rows_ref, data_ref, other_ref, sums_ref, peaks_ref, totals_ref, out_ref, acc_ref):
    def emit(s, mixed, top, total):
        shrink = jnp.exp2(peaks_ref[s : s + 1, :] - top)
        total = total + totals_ref[s : s + 1, :] * shrink
        rows = ((mixed + sums_ref[s] * shrink) * (1.0 / total)).T
        for h in range(GROUP_HEADS):
            for y in range(4):
                at = h * PART + y * BR
                acc_ref[y, s * BR : (s + 1) * BR, h * HEAD : (h + 1) * HEAD] = rows[at : at + BR]

    attend_half(1, rows_ref, data_ref, other_ref, 0, sums_ref, peaks_ref, totals_ref, emit)
    out_ref[...] = acc_ref[...].astype(jnp.bfloat16)


def unpack_kernel(in_ref, out_any, sems):
    wide = GROUP_HEADS * HEAD
    copies = [
        pltpu.make_async_copy(in_ref.at[g], out_any.at[:, g * wide : (g + 1) * wide], sems.at[g])
        for g in range(GROUPS)
    ]
    for copy in copies:
        copy.start()
    for copy in copies:
        copy.wait()


VMEM = pl.BlockSpec(memory_space=pltpu.VMEM)
ANY = pl.BlockSpec(memory_space=pl.ANY)


def body(queries, keys, values, doc_lengths, owner_map):
    here = [
        pltpu.with_memory_space_constraint(a, pltpu.HBM)
        for a in (owner_map, doc_lengths, queries, keys, values)
    ]
    packed, rows = pl.pallas_call(
        pack_kernel,
        out_shape=(
            jax.ShapeDtypeStruct((CTX, CHUNK, HEAD), jnp.bfloat16),
            jax.ShapeDtypeStruct((2, CTX, TOK), jnp.int32),
        ),
        in_specs=[ANY] * 5,
        out_specs=(VMEM, VMEM),
        scratch_shapes=[
            pltpu.SMEM((CTX, CTX), jnp.int32),
            pltpu.VMEM((CTX, CTX), jnp.int32),
            pltpu.SMEM((NDOC,), jnp.int32),
            pltpu.VMEM(queries.shape, jnp.bfloat16),
            pltpu.VMEM(keys.shape, jnp.bfloat16),
            pltpu.VMEM(values.shape, jnp.bfloat16),
            pltpu.SemaphoreType.DMA((6,)),
        ],
        compiler_params=pltpu.CompilerParams(vmem_limit_bytes=24 << 20),
        name="pack",
    )(*here)
    data = lax.all_to_all(packed, "ctx", 0, 0, tiled=True)
    other = lax.ppermute(data[:, TOK:], "ctx", [(i, i ^ 1) for i in range(CTX)])
    sums, peaks, totals = pl.pallas_call(
        own_kernel,
        out_shape=(
            jax.ShapeDtypeStruct((CTX, HEAD, TOK), jnp.float32),
            jax.ShapeDtypeStruct((CTX, TOK), jnp.float32),
            jax.ShapeDtypeStruct((CTX, TOK), jnp.float32),
        ),
        in_specs=[VMEM] * 2,
        out_specs=(VMEM,) * 3,
        compiler_params=pltpu.CompilerParams(vmem_limit_bytes=40 << 20),
        cost_estimate=pl.CostEstimate(flops=10**9, bytes_accessed=3 << 20, transcendentals=10**6),
        name="own_half",
    )(rows, data)
    mixed = pl.pallas_call(
        other_kernel,
        out_shape=jax.ShapeDtypeStruct((4, TOK, GROUP_HEADS * HEAD), jnp.bfloat16),
        in_specs=[VMEM] * 6,
        out_specs=VMEM,
        scratch_shapes=[pltpu.VMEM((4, TOK, GROUP_HEADS * HEAD), jnp.float32)],
        compiler_params=pltpu.CompilerParams(vmem_limit_bytes=40 << 20),
        name="other_half",
    )(rows, data, other, sums, peaks, totals)
    rings = [[x * 8 + y * 2 + c for y in range(4)] for x in range(2) for c in range(2)]
    back = lax.all_to_all(mixed, "ctx", 0, 0, tiled=True, axis_index_groups=rings)
    return pl.pallas_call(
        unpack_kernel,
        out_shape=jax.ShapeDtypeStruct(queries.shape, jnp.bfloat16),
        in_specs=[VMEM],
        out_specs=ANY,
        scratch_shapes=[pltpu.SemaphoreType.DMA((GROUPS,))],
        compiler_params=pltpu.CompilerParams(vmem_limit_bytes=16 << 20),
        name="unpack",
    )(back)


def solution(mesh):
    placed = (
        P(("dp", "ctx"), "head"),
        P(("dp", "ctx"), "head"),
        P(("dp", "ctx"), "head"),
        P("dp"),
        P("dp", None),
    )
    return jax.shard_map(
        body, mesh=mesh, in_specs=placed, out_specs=P(("dp", "ctx"), "head"), check_vma=False
    )
```

```python
import math

import jax
import jax.numpy as jnp
from jax import lax
from jax.experimental import pallas as pl
from jax.experimental.pallas import tpu as pltpu
from jax.sharding import PartitionSpec as P

HEAD = 128
CTX = 16
TOK = 128
BR = 8
NDOC = 16
GROUPS = 4
GROUP_HEADS = 4
PART = 32
REACH = 8
CHUNK = 256
MASKED = -1e30
ORDER = [5, 6, 10, 11, 8, 4, 7, 0, 1, 15, 2, 3, 13, 14, 9, 12]
PLACE = [ORDER.index(i) for i in range(CTX)]
RING = [2, 0, 3, 1]
SPOT = [RING.index(y) for y in range(4)]
SCALE = math.log2(math.e) / math.sqrt(HEAD)
ROWS_BY_ROWS = (((1,), (1,)), ((), ()))
ROWS_BY_COLS = (((1,), (0,)), ((), ()))


def dot(a, b, dims):
    return lax.dot_general(a, b, dims, preferred_element_type=jnp.float32)


def pack_kernel(owner_any, doc_any, q_any, k_any, v_any, out_ref, rows_ref, owner_ref, owners_ref, doc_ref, q_ref, k_ref, v_ref, sems):
    me = lax.axis_index("ctx")
    moves = (
        (owner_any, owner_ref),
        (owner_any, owners_ref),
        (doc_any, doc_ref),
        (k_any, k_ref),
        (v_any, v_ref),
        (q_any, q_ref),
    )
    copies = [pltpu.make_async_copy(src, dst, sems.at[i]) for i, (src, dst) in enumerate(moves)]
    for copy in copies:
        copy.start()
    for copy in copies[:3]:
        copy.wait()
    one_lane = lax.broadcasted_iota(jnp.int32, (1, TOK), 1)
    goal = one_lane % BR
    for b in range(CTX):
        owner = owner_ref[me, b]
        rank = ((owner // 8) * 2 + owner % 2) * 4 + (owner // 2) % 4
        goal = goal + jnp.where(one_lane // BR == b, rank * BR, 0)
    row = lax.broadcasted_iota(jnp.int32, (TOK, TOK), 0)
    order = jnp.where(row == goal, 1.0, 0.0).astype(jnp.bfloat16)

    lane = lax.broadcasted_iota(jnp.int32, (CTX, TOK), 1)
    shard = lax.broadcasted_iota(jnp.int32, (CTX, TOK), 0)
    mine = (me // 8) * 8 + ((lane // BR) % 4) * 2 + me % 2
    owners = owners_ref[...]
    pos = shard * TOK + lane % BR
    for b in range(CTX):
        pos = pos + jnp.where(owners[:, b : b + 1] == mine, b * BR, 0)
    start = jnp.zeros((CTX, TOK), jnp.int32)
    end = jnp.int32(0)
    for n in range(NDOC - 1):
        end = end + doc_ref[n]
        start = jnp.where(pos >= end, end, start)
    rows_ref[0] = pos
    rows_ref[1] = start

    for copy in copies[3:5]:
        copy.wait()
    for g in range(GROUPS):
        cols = slice(g * HEAD, (g + 1) * HEAD)
        keys = k_ref[:, cols]
        vals = v_ref[:, cols]
        for part in range(4):
            dest = PLACE[(part // 2) * 8 + g * 2 + part % 2]
            half = slice(part % 2 * 64, part % 2 * 64 + 64)
            out_ref[dest, 128:192, :] = keys[half]
            out_ref[dest, 192:256, :] = vals[half]
    copies[5].wait()
    for g in range(GROUPS):
        wide = slice(g * GROUP_HEADS * HEAD, (g + 1) * GROUP_HEADS * HEAD)
        moved = dot(order, q_ref[:, wide], ROWS_BY_COLS).astype(jnp.bfloat16)
        for part in range(4):
            dest = PLACE[(part // 2) * 8 + g * 2 + part % 2]
            for h in range(GROUP_HEADS):
                out_ref[dest, h * PART : (h + 1) * PART, :] = moved[
                    part * PART : (part + 1) * PART, h * HEAD : (h + 1) * HEAD
                ]


def attend_half(second, rows_ref, data_ref, half_ref, offset, sums_ref, peaks_ref, totals_ref, emit):
    half = (lax.axis_index("ctx") + second) % 2
    row = lax.broadcasted_iota(jnp.int32, (TOK, TOK), 0)
    key_at = (row // 64) * TOK + row % 64 + half * 64

    def two(ref, m, low, high):
        return jnp.concatenate([ref[PLACE[2 * m], low:high, :], ref[PLACE[2 * m + 1], low:high, :]], 0)

    def keys(m):
        return two(half_ref, m, offset, offset + 64)

    def values(m):
        return two(half_ref, m, offset + 64, offset + 128).T

    turned = [values(m) for m in range(CTX // 2)]

    def scores(pair):
        tiles = range(max(0, pair - REACH // 2), pair + 1)
        q = two(data_ref, pair, 0, 128)
        kept = []
        peak = [None, None]
        for m in tiles:
            both = dot(keys(m), q, ROWS_BY_ROWS)
            ones = []
            for i in range(2):
                s = 2 * pair + i
                one = both[:, i * TOK : (i + 1) * TOK]
                seen = key_at >= rows_ref[1, s : s + 1, :] - m * 2 * TOK
                if m == pair:
                    seen = seen & (key_at <= rows_ref[0, s : s + 1, :] - m * 2 * TOK)
                one = jnp.where(seen, one, MASKED)
                ones.append(one)
                top = jnp.max(one.reshape(16, 8, TOK), axis=0)
                peak[i] = top if peak[i] is None else jnp.maximum(peak[i], top)
            kept.append(ones)
        return pair, tiles, kept, peak

    def finish(state):
        pair, tiles, kept, peak = state
        tops, totals = [], []
        for i in range(2):
            top = jnp.max(peak[i], axis=0, keepdims=True) * SCALE
            if second:
                top = jnp.maximum(top, peaks_ref[2 * pair + i : 2 * pair + i + 1, :])
            tops.append(top)
            totals.append(jnp.zeros((8, TOK), jnp.float32))
        wide = []
        for ones in kept:
            parts = []
            for i in range(2):
                w = jnp.exp2(ones[i] * SCALE - tops[i])
                totals[i] = totals[i] + jnp.sum(w.reshape(16, 8, TOK), axis=0)
                parts.append(w.astype(jnp.bfloat16))
            wide.append(jnp.concatenate(parts, 1))
        mixed = dot(
            jnp.concatenate([turned[m] for m in tiles], 1), jnp.concatenate(wide, 0), ROWS_BY_COLS
        )
        for i in range(2):
            total = jnp.sum(totals[i], axis=0, keepdims=True)
            emit(2 * pair + i, mixed[:, i * TOK : (i + 1) * TOK], tops[i], total)

    ahead = scores(0)
    for pair in range(1, CTX // 2):
        following = scores(pair)
        finish(ahead)
        ahead = following
    finish(ahead)


def own_kernel(rows_ref, data_ref, sums_ref, peaks_ref, totals_ref):
    def emit(s, mixed, top, total):
        sums_ref[s] = mixed
        peaks_ref[s : s + 1, :] = top
        totals_ref[s : s + 1, :] = total

    attend_half(0, rows_ref, data_ref, data_ref, TOK, None, None, None, emit)


def other_kernel(rows_ref, data_ref, other_ref, sums_ref, peaks_ref, totals_ref, out_ref, acc_ref):
    def emit(s, mixed, top, total):
        shrink = jnp.exp2(peaks_ref[s : s + 1, :] - top)
        total = total + totals_ref[s : s + 1, :] * shrink
        rows = ((mixed + sums_ref[s] * shrink) * (1.0 / total)).T
        for h in range(GROUP_HEADS):
            for y in range(4):
                at = h * PART + y * BR
                acc_ref[SPOT[y], s * BR : (s + 1) * BR, h * HEAD : (h + 1) * HEAD] = rows[at : at + BR]

    attend_half(1, rows_ref, data_ref, other_ref, 0, sums_ref, peaks_ref, totals_ref, emit)
    out_ref[...] = acc_ref[...].astype(jnp.bfloat16)


def unpack_kernel(in_ref, out_any, sems):
    wide = GROUP_HEADS * HEAD
    copies = [
        pltpu.make_async_copy(in_ref.at[SPOT[g]], out_any.at[:, g * wide : (g + 1) * wide], sems.at[g])
        for g in range(GROUPS)
    ]
    for copy in copies:
        copy.start()
    for copy in copies:
        copy.wait()


VMEM = pl.BlockSpec(memory_space=pltpu.VMEM)
ANY = pl.BlockSpec(memory_space=pl.ANY)


def body(queries, keys, values, doc_lengths, owner_map):
    here = [
        pltpu.with_memory_space_constraint(a, pltpu.HBM)
        for a in (owner_map, doc_lengths, queries, keys, values)
    ]
    packed, rows = pl.pallas_call(
        pack_kernel,
        out_shape=(
            jax.ShapeDtypeStruct((CTX, CHUNK, HEAD), jnp.bfloat16),
            jax.ShapeDtypeStruct((2, CTX, TOK), jnp.int32),
        ),
        in_specs=[ANY] * 5,
        out_specs=(VMEM, VMEM),
        scratch_shapes=[
            pltpu.SMEM((CTX, CTX), jnp.int32),
            pltpu.VMEM((CTX, CTX), jnp.int32),
            pltpu.SMEM((NDOC,), jnp.int32),
            pltpu.VMEM(queries.shape, jnp.bfloat16),
            pltpu.VMEM(keys.shape, jnp.bfloat16),
            pltpu.VMEM(values.shape, jnp.bfloat16),
            pltpu.SemaphoreType.DMA((6,)),
        ],
        compiler_params=pltpu.CompilerParams(vmem_limit_bytes=24 << 20),
        name="pack",
    )(*here)
    data = lax.all_to_all(packed, "ctx", 0, 0, tiled=True, axis_index_groups=[ORDER])
    other = lax.ppermute(data[:, TOK:], "ctx", [(i, i ^ 1) for i in range(CTX)])
    sums, peaks, totals = pl.pallas_call(
        own_kernel,
        out_shape=(
            jax.ShapeDtypeStruct((CTX, HEAD, TOK), jnp.float32),
            jax.ShapeDtypeStruct((CTX, TOK), jnp.float32),
            jax.ShapeDtypeStruct((CTX, TOK), jnp.float32),
        ),
        in_specs=[VMEM] * 2,
        out_specs=(VMEM,) * 3,
        compiler_params=pltpu.CompilerParams(vmem_limit_bytes=40 << 20),
        cost_estimate=pl.CostEstimate(flops=10**9, bytes_accessed=3 << 20, transcendentals=10**6),
        name="own_half",
    )(rows, data)
    mixed = pl.pallas_call(
        other_kernel,
        out_shape=jax.ShapeDtypeStruct((4, TOK, GROUP_HEADS * HEAD), jnp.bfloat16),
        in_specs=[VMEM] * 6,
        out_specs=VMEM,
        scratch_shapes=[pltpu.VMEM((4, TOK, GROUP_HEADS * HEAD), jnp.float32)],
        compiler_params=pltpu.CompilerParams(vmem_limit_bytes=40 << 20),
        name="other_half",
    )(rows, data, other, sums, peaks, totals)
    rings = [[x * 8 + y * 2 + c for y in RING] for x in range(2) for c in range(2)]
    back = lax.all_to_all(mixed, "ctx", 0, 0, tiled=True, axis_index_groups=rings)
    return pl.pallas_call(
        unpack_kernel,
        out_shape=jax.ShapeDtypeStruct(queries.shape, jnp.bfloat16),
        in_specs=[VMEM],
        out_specs=ANY,
        scratch_shapes=[pltpu.SemaphoreType.DMA((GROUPS,))],
        compiler_params=pltpu.CompilerParams(vmem_limit_bytes=16 << 20),
        name="unpack",
    )(back)


def solution(mesh):
    placed = (
        P(("dp", "ctx"), "head"),
        P(("dp", "ctx"), "head"),
        P(("dp", "ctx"), "head"),
        P("dp"),
        P("dp", None),
    )
    return jax.shard_map(
        body, mesh=mesh, in_specs=placed, out_specs=P(("dp", "ctx"), "head"), check_vma=False
    )
```

```python
import math

import jax
import jax.numpy as jnp
from jax import lax
from jax.experimental import pallas as pl
from jax.experimental.pallas import tpu as pltpu
from jax.sharding import PartitionSpec as P

HEAD = 128
CTX = 16
TOK = 128
BR = 8
NDOC = 16
GROUPS = 4
GROUP_HEADS = 4
PART = 32
REACH = 8
CHUNK = 256
MASKED = -1e30
ORDER = [5, 6, 10, 11, 8, 4, 7, 0, 1, 15, 2, 3, 13, 14, 9, 12]
PLACE = [ORDER.index(i) for i in range(CTX)]
RING = [2, 0, 3, 1]
SPOT = [RING.index(y) for y in range(4)]
SCALE = math.log2(math.e) / math.sqrt(HEAD)
ROWS_BY_ROWS = (((1,), (1,)), ((), ()))
ROWS_BY_COLS = (((1,), (0,)), ((), ()))


def dot(a, b, dims):
    return lax.dot_general(a, b, dims, preferred_element_type=jnp.float32)


def pack_kernel(owner_any, doc_any, q_any, k_any, v_any, out_ref, rows_ref, owner_ref, owners_ref, doc_ref, q_ref, k_ref, v_ref, sems):
    me = lax.axis_index("ctx")
    moves = (
        (owner_any, owner_ref),
        (owner_any, owners_ref),
        (doc_any, doc_ref),
        (k_any, k_ref),
        (v_any, v_ref),
        (q_any, q_ref),
    )
    copies = [pltpu.make_async_copy(src, dst, sems.at[i]) for i, (src, dst) in enumerate(moves)]
    for copy in copies:
        copy.start()
    for copy in copies[:3]:
        copy.wait()
    one_lane = lax.broadcasted_iota(jnp.int32, (1, TOK), 1)
    goal = one_lane % BR
    for b in range(CTX):
        owner = owner_ref[me, b]
        rank = ((owner // 8) * 2 + owner % 2) * 4 + (owner // 2) % 4
        goal = goal + jnp.where(one_lane // BR == b, rank * BR, 0)
    row = lax.broadcasted_iota(jnp.int32, (TOK, TOK), 0)
    order = jnp.where(row == goal, 1.0, 0.0).astype(jnp.bfloat16)

    lane = lax.broadcasted_iota(jnp.int32, (CTX, TOK), 1)
    shard = lax.broadcasted_iota(jnp.int32, (CTX, TOK), 0)
    mine = (me // 8) * 8 + ((lane // BR) % 4) * 2 + me % 2
    owners = owners_ref[...]
    pos = shard * TOK + lane % BR
    for b in range(CTX):
        pos = pos + jnp.where(owners[:, b : b + 1] == mine, b * BR, 0)
    start = jnp.zeros((CTX, TOK), jnp.int32)
    end = jnp.int32(0)
    for n in range(NDOC - 1):
        end = end + doc_ref[n]
        start = jnp.where(pos >= end, end, start)
    rows_ref[0] = pos
    rows_ref[1] = start

    for copy in copies[3:5]:
        copy.wait()
    for g in range(GROUPS):
        cols = slice(g * HEAD, (g + 1) * HEAD)
        keys = k_ref[:, cols]
        vals = v_ref[:, cols]
        for part in range(4):
            dest = PLACE[(part // 2) * 8 + g * 2 + part % 2]
            half = slice(part % 2 * 64, part % 2 * 64 + 64)
            out_ref[dest, 128:192, :] = keys[half]
            out_ref[dest, 192:256, :] = vals[half]
    copies[5].wait()
    for g in range(GROUPS):
        wide = slice(g * GROUP_HEADS * HEAD, (g + 1) * GROUP_HEADS * HEAD)
        moved = dot(order, q_ref[:, wide], ROWS_BY_COLS).astype(jnp.bfloat16)
        for part in range(4):
            dest = PLACE[(part // 2) * 8 + g * 2 + part % 2]
            for h in range(GROUP_HEADS):
                out_ref[dest, h * PART : (h + 1) * PART, :] = moved[
                    part * PART : (part + 1) * PART, h * HEAD : (h + 1) * HEAD
                ]


def attend_half(second, rows_ref, data_ref, half_ref, offset, sums_ref, peaks_ref, totals_ref, emit):
    half = (lax.axis_index("ctx") + second) % 2
    row = lax.broadcasted_iota(jnp.int32, (TOK, TOK), 0)
    key_at = (row // 64) * TOK + row % 64 + half * 64

    def two(ref, m, low, high):
        return jnp.concatenate([ref[PLACE[2 * m], low:high, :], ref[PLACE[2 * m + 1], low:high, :]], 0)

    def keys(m):
        return two(half_ref, m, offset, offset + 64)

    def values(m):
        return two(half_ref, m, offset + 64, offset + 128).T

    turned = [values(m) for m in range(CTX // 2)]

    def reached(pair, m, i):
        if m == pair and i == 0:
            return slice(0, 64)
        if m == pair - REACH // 2 and i == 1:
            return slice(64, TOK)
        return slice(0, TOK)

    def scores(pair):
        tiles = range(max(0, pair - REACH // 2), pair + 1)
        q = two(data_ref, pair, 0, 128)
        kept = []
        peak = [None, None]
        for m in tiles:
            both = dot(keys(m), q, ROWS_BY_ROWS)
            ones = []
            for i in range(2):
                s = 2 * pair + i
                part = reached(pair, m, i)
                one = both[part, i * TOK : (i + 1) * TOK]
                seen = key_at[part] >= rows_ref[1, s : s + 1, :] - m * 2 * TOK
                if m == pair:
                    seen = seen & (key_at[part] <= rows_ref[0, s : s + 1, :] - m * 2 * TOK)
                one = jnp.where(seen, one, MASKED)
                ones.append(one)
                top = jnp.max(one.reshape(-1, 8, TOK), axis=0)
                peak[i] = top if peak[i] is None else jnp.maximum(peak[i], top)
            kept.append(ones)
        return pair, tiles, kept, peak

    def finish(state):
        pair, tiles, kept, peak = state
        tops, totals = [], []
        for i in range(2):
            top = jnp.max(peak[i], axis=0, keepdims=True) * SCALE
            if second:
                top = jnp.maximum(top, peaks_ref[2 * pair + i : 2 * pair + i + 1, :])
            tops.append(top)
            totals.append(jnp.zeros((8, TOK), jnp.float32))
        wide = []
        none = jnp.zeros((64, TOK), jnp.bfloat16)
        for m, ones in zip(tiles, kept):
            parts = []
            for i in range(2):
                w = jnp.exp2(ones[i] * SCALE - tops[i])
                totals[i] = totals[i] + jnp.sum(w.reshape(-1, 8, TOK), axis=0)
                w = w.astype(jnp.bfloat16)
                part = reached(pair, m, i)
                if part.start > 0:
                    w = jnp.concatenate([none, w], 0)
                if part.stop < TOK:
                    w = jnp.concatenate([w, none], 0)
                parts.append(w)
            wide.append(jnp.concatenate(parts, 1))
        mixed = dot(
            jnp.concatenate([turned[m] for m in tiles], 1), jnp.concatenate(wide, 0), ROWS_BY_COLS
        )
        for i in range(2):
            total = jnp.sum(totals[i], axis=0, keepdims=True)
            emit(2 * pair + i, mixed[:, i * TOK : (i + 1) * TOK], tops[i], total)

    ahead = scores(0)
    for pair in range(1, CTX // 2):
        following = scores(pair)
        finish(ahead)
        ahead = following
    finish(ahead)


def own_kernel(rows_ref, data_ref, sums_ref, peaks_ref, totals_ref):
    def emit(s, mixed, top, total):
        sums_ref[s] = mixed
        peaks_ref[s : s + 1, :] = top
        totals_ref[s : s + 1, :] = total

    attend_half(0, rows_ref, data_ref, data_ref, TOK, None, None, None, emit)


def other_kernel(rows_ref, data_ref, other_ref, sums_ref, peaks_ref, totals_ref, out_ref, acc_ref):
    def emit(s, mixed, top, total):
        shrink = jnp.exp2(peaks_ref[s : s + 1, :] - top)
        total = total + totals_ref[s : s + 1, :] * shrink
        rows = ((mixed + sums_ref[s] * shrink) * (1.0 / total)).T
        for h in range(GROUP_HEADS):
            for y in range(4):
                at = h * PART + y * BR
                acc_ref[SPOT[y], s * BR : (s + 1) * BR, h * HEAD : (h + 1) * HEAD] = rows[at : at + BR]

    attend_half(1, rows_ref, data_ref, other_ref, 0, sums_ref, peaks_ref, totals_ref, emit)
    out_ref[...] = acc_ref[...].astype(jnp.bfloat16)


def unpack_kernel(in_ref, out_any, sems):
    wide = GROUP_HEADS * HEAD
    copies = [
        pltpu.make_async_copy(in_ref.at[SPOT[g]], out_any.at[:, g * wide : (g + 1) * wide], sems.at[g])
        for g in range(GROUPS)
    ]
    for copy in copies:
        copy.start()
    for copy in copies:
        copy.wait()


VMEM = pl.BlockSpec(memory_space=pltpu.VMEM)
ANY = pl.BlockSpec(memory_space=pl.ANY)


def body(queries, keys, values, doc_lengths, owner_map):
    here = [
        pltpu.with_memory_space_constraint(a, pltpu.HBM)
        for a in (owner_map, doc_lengths, queries, keys, values)
    ]
    packed, rows = pl.pallas_call(
        pack_kernel,
        out_shape=(
            jax.ShapeDtypeStruct((CTX, CHUNK, HEAD), jnp.bfloat16),
            jax.ShapeDtypeStruct((2, CTX, TOK), jnp.int32),
        ),
        in_specs=[ANY] * 5,
        out_specs=(VMEM, VMEM),
        scratch_shapes=[
            pltpu.SMEM((CTX, CTX), jnp.int32),
            pltpu.VMEM((CTX, CTX), jnp.int32),
            pltpu.SMEM((NDOC,), jnp.int32),
            pltpu.VMEM(queries.shape, jnp.bfloat16),
            pltpu.VMEM(keys.shape, jnp.bfloat16),
            pltpu.VMEM(values.shape, jnp.bfloat16),
            pltpu.SemaphoreType.DMA((6,)),
        ],
        compiler_params=pltpu.CompilerParams(vmem_limit_bytes=24 << 20),
        name="pack",
    )(*here)
    data = lax.all_to_all(packed, "ctx", 0, 0, tiled=True, axis_index_groups=[ORDER])
    other = lax.ppermute(data[:, TOK:], "ctx", [(i, i ^ 1) for i in range(CTX)])
    sums, peaks, totals = pl.pallas_call(
        own_kernel,
        out_shape=(
            jax.ShapeDtypeStruct((CTX, HEAD, TOK), jnp.float32),
            jax.ShapeDtypeStruct((CTX, TOK), jnp.float32),
            jax.ShapeDtypeStruct((CTX, TOK), jnp.float32),
        ),
        in_specs=[VMEM] * 2,
        out_specs=(VMEM,) * 3,
        compiler_params=pltpu.CompilerParams(vmem_limit_bytes=40 << 20),
        cost_estimate=pl.CostEstimate(flops=10**9, bytes_accessed=3 << 20, transcendentals=10**6),
        name="own_half",
    )(rows, data)
    mixed = pl.pallas_call(
        other_kernel,
        out_shape=jax.ShapeDtypeStruct((4, TOK, GROUP_HEADS * HEAD), jnp.bfloat16),
        in_specs=[VMEM] * 6,
        out_specs=VMEM,
        scratch_shapes=[pltpu.VMEM((4, TOK, GROUP_HEADS * HEAD), jnp.float32)],
        compiler_params=pltpu.CompilerParams(vmem_limit_bytes=40 << 20),
        name="other_half",
    )(rows, data, other, sums, peaks, totals)
    rings = [[x * 8 + y * 2 + c for y in RING] for x in range(2) for c in range(2)]
    back = lax.all_to_all(mixed, "ctx", 0, 0, tiled=True, axis_index_groups=rings)
    return pl.pallas_call(
        unpack_kernel,
        out_shape=jax.ShapeDtypeStruct(queries.shape, jnp.bfloat16),
        in_specs=[VMEM],
        out_specs=ANY,
        scratch_shapes=[pltpu.SemaphoreType.DMA((GROUPS,))],
        compiler_params=pltpu.CompilerParams(vmem_limit_bytes=16 << 20),
        name="unpack",
    )(back)


def solution(mesh):
    placed = (
        P(("dp", "ctx"), "head"),
        P(("dp", "ctx"), "head"),
        P(("dp", "ctx"), "head"),
        P("dp"),
        P("dp", None),
    )
    return jax.shard_map(
        body, mesh=mesh, in_specs=placed, out_specs=P(("dp", "ctx"), "head"), check_vma=False
    )
```

```python
import math

import jax
import jax.numpy as jnp
from jax import lax
from jax.experimental import pallas as pl
from jax.experimental.pallas import tpu as pltpu
from jax.sharding import PartitionSpec as P

HEAD = 128
CTX = 16
TOK = 128
BR = 8
NDOC = 16
GROUPS = 4
GROUP_HEADS = 4
PART = 32
REACH = 8
CHUNK = 256
MASKED = -1e30
ORDER = [5, 6, 10, 11, 8, 4, 7, 0, 1, 15, 2, 3, 13, 14, 9, 12]
PLACE = [ORDER.index(i) for i in range(CTX)]
RING = [2, 0, 3, 1]
SPOT = [RING.index(y) for y in range(4)]
SCALE = math.log2(math.e) / math.sqrt(HEAD)
ROWS_BY_ROWS = (((1,), (1,)), ((), ()))
ROWS_BY_COLS = (((1,), (0,)), ((), ()))


def dot(a, b, dims):
    return lax.dot_general(a, b, dims, preferred_element_type=jnp.float32)


def pack_kernel(owner_any, doc_any, q_any, k_any, v_any, out_ref, rows_ref, owner_ref, owners_ref, doc_ref, q_ref, k_ref, v_ref, sems):
    me = lax.axis_index("ctx")
    moves = (
        (owner_any, owner_ref),
        (owner_any, owners_ref),
        (doc_any, doc_ref),
        (k_any, k_ref),
        (v_any, v_ref),
        (q_any, q_ref),
    )
    copies = [pltpu.make_async_copy(src, dst, sems.at[i]) for i, (src, dst) in enumerate(moves)]
    for copy in copies:
        copy.start()
    for copy in copies[:3]:
        copy.wait()
    one_lane = lax.broadcasted_iota(jnp.int32, (1, TOK), 1)
    goal = one_lane % BR
    for b in range(CTX):
        owner = owner_ref[me, b]
        rank = ((owner // 8) * 2 + owner % 2) * 4 + (owner // 2) % 4
        goal = goal + jnp.where(one_lane // BR == b, rank * BR, 0)
    row = lax.broadcasted_iota(jnp.int32, (TOK, TOK), 0)
    order = jnp.where(row == goal, 1.0, 0.0).astype(jnp.bfloat16)

    lane = lax.broadcasted_iota(jnp.int32, (CTX, TOK), 1)
    shard = lax.broadcasted_iota(jnp.int32, (CTX, TOK), 0)
    mine = (me // 8) * 8 + ((lane // BR) % 4) * 2 + me % 2
    owners = owners_ref[...]
    pos = shard * TOK + lane % BR
    for b in range(CTX):
        pos = pos + jnp.where(owners[:, b : b + 1] == mine, b * BR, 0)
    start = jnp.zeros((CTX, TOK), jnp.int32)
    end = jnp.int32(0)
    for n in range(NDOC - 1):
        end = end + doc_ref[n]
        start = jnp.where(pos >= end, end, start)
    rows_ref[0] = pos
    rows_ref[1] = start

    for copy in copies[3:5]:
        copy.wait()
    for g in range(GROUPS):
        cols = slice(g * HEAD, (g + 1) * HEAD)
        keys = k_ref[:, cols]
        vals = v_ref[:, cols]
        for part in range(4):
            dest = PLACE[(part // 2) * 8 + g * 2 + part % 2]
            half = slice(part % 2 * 64, part % 2 * 64 + 64)
            out_ref[dest, 128:192, :] = keys[half]
            out_ref[dest, 192:256, :] = vals[half]
    copies[5].wait()
    for g in range(GROUPS):
        wide = slice(g * GROUP_HEADS * HEAD, (g + 1) * GROUP_HEADS * HEAD)
        moved = dot(order, q_ref[:, wide], ROWS_BY_COLS).astype(jnp.bfloat16)
        for part in range(4):
            dest = PLACE[(part // 2) * 8 + g * 2 + part % 2]
            for h in range(GROUP_HEADS):
                out_ref[dest, h * PART : (h + 1) * PART, :] = moved[
                    part * PART : (part + 1) * PART, h * HEAD : (h + 1) * HEAD
                ]


def attend_half(second, rows_ref, data_ref, half_ref, offset, sums_ref, peaks_ref, totals_ref, emit):
    half = (lax.axis_index("ctx") + second) % 2
    row = lax.broadcasted_iota(jnp.int32, (TOK, TOK), 0)
    key_at = (row // 64) * TOK + row % 64 + half * 64

    def two(ref, m, low, high):
        return jnp.concatenate([ref[PLACE[2 * m], low:high, :], ref[PLACE[2 * m + 1], low:high, :]], 0)

    def keys(m):
        return two(half_ref, m, offset, offset + 64)

    def values(m):
        return two(half_ref, m, offset + 64, offset + 128).T

    turned = [values(m) for m in range(CTX // 2)]

    def reached(pair, m, i):
        if m == pair and i == 0:
            return slice(0, 64)
        if m == pair - REACH // 2 and i == 1:
            return slice(64, TOK)
        return slice(0, TOK)

    def scores(pair):
        tiles = range(max(0, pair - REACH // 2), pair + 1)
        q = two(data_ref, pair, 0, 128)
        kept = []
        peak = [None, None]
        for m in tiles:
            both = dot(keys(m), q, ROWS_BY_ROWS)
            ones = []
            for i in range(2):
                s = 2 * pair + i
                part = reached(pair, m, i)
                one = both[part, i * TOK : (i + 1) * TOK]
                seen = key_at[part] >= rows_ref[1, s : s + 1, :] - m * 2 * TOK
                if m == pair:
                    seen = seen & (key_at[part] <= rows_ref[0, s : s + 1, :] - m * 2 * TOK)
                one = jnp.where(seen, one, MASKED)
                ones.append(one)
                top = jnp.max(one.reshape(-1, 8, TOK), axis=0)
                peak[i] = top if peak[i] is None else jnp.maximum(peak[i], top)
            kept.append(ones)
        return pair, tiles, kept, peak

    def finish(state):
        pair, tiles, kept, peak = state
        tops, totals = [], []
        for i in range(2):
            top = jnp.max(peak[i], axis=0, keepdims=True) * SCALE
            if second:
                top = jnp.maximum(top, peaks_ref[2 * pair + i : 2 * pair + i + 1, :])
            tops.append(top)
            totals.append(jnp.zeros((8, TOK), jnp.float32))
        wide = []
        none = jnp.zeros((64, TOK), jnp.bfloat16)
        for m, ones in zip(tiles, kept):
            parts = []
            for i in range(2):
                w = jnp.exp2(ones[i] * SCALE - tops[i])
                totals[i] = totals[i] + jnp.sum(w.reshape(-1, 8, TOK), axis=0)
                w = w.astype(jnp.bfloat16)
                part = reached(pair, m, i)
                if part.start > 0:
                    w = jnp.concatenate([none, w], 0)
                if part.stop < TOK:
                    w = jnp.concatenate([w, none], 0)
                parts.append(w)
            wide.append(jnp.concatenate(parts, 1))
        mixed = dot(
            jnp.concatenate([turned[m] for m in tiles], 1), jnp.concatenate(wide, 0), ROWS_BY_COLS
        )
        for i in range(2):
            total = jnp.sum(totals[i], axis=0, keepdims=True)
            emit(2 * pair + i, mixed[:, i * TOK : (i + 1) * TOK], tops[i], total)

    order = (1, 3, 5, 7, 6, 4, 2, 0)
    ahead = scores(order[0])
    for pair in order[1:]:
        following = scores(pair)
        finish(ahead)
        ahead = following
    finish(ahead)


def own_kernel(rows_ref, data_ref, sums_ref, peaks_ref, totals_ref):
    def emit(s, mixed, top, total):
        sums_ref[s] = mixed
        peaks_ref[s : s + 1, :] = top
        totals_ref[s : s + 1, :] = total

    attend_half(0, rows_ref, data_ref, data_ref, TOK, None, None, None, emit)


def other_kernel(rows_ref, data_ref, other_ref, sums_ref, peaks_ref, totals_ref, out_ref, acc_ref):
    def emit(s, mixed, top, total):
        shrink = jnp.exp2(peaks_ref[s : s + 1, :] - top)
        total = total + totals_ref[s : s + 1, :] * shrink
        rows = ((mixed + sums_ref[s] * shrink) * (1.0 / total)).T
        for h in range(GROUP_HEADS):
            for y in range(4):
                at = h * PART + y * BR
                acc_ref[SPOT[y], s * BR : (s + 1) * BR, h * HEAD : (h + 1) * HEAD] = rows[at : at + BR]

    attend_half(1, rows_ref, data_ref, other_ref, 0, sums_ref, peaks_ref, totals_ref, emit)
    out_ref[...] = acc_ref[...].astype(jnp.bfloat16)


def unpack_kernel(in_ref, out_any, sems):
    wide = GROUP_HEADS * HEAD
    copies = [
        pltpu.make_async_copy(in_ref.at[SPOT[g]], out_any.at[:, g * wide : (g + 1) * wide], sems.at[g])
        for g in range(GROUPS)
    ]
    for copy in copies:
        copy.start()
    for copy in copies:
        copy.wait()


VMEM = pl.BlockSpec(memory_space=pltpu.VMEM)
ANY = pl.BlockSpec(memory_space=pl.ANY)


def body(queries, keys, values, doc_lengths, owner_map):
    here = [
        pltpu.with_memory_space_constraint(a, pltpu.HBM)
        for a in (owner_map, doc_lengths, queries, keys, values)
    ]
    packed, rows = pl.pallas_call(
        pack_kernel,
        out_shape=(
            jax.ShapeDtypeStruct((CTX, CHUNK, HEAD), jnp.bfloat16),
            jax.ShapeDtypeStruct((2, CTX, TOK), jnp.int32),
        ),
        in_specs=[ANY] * 5,
        out_specs=(VMEM, VMEM),
        scratch_shapes=[
            pltpu.SMEM((CTX, CTX), jnp.int32),
            pltpu.VMEM((CTX, CTX), jnp.int32),
            pltpu.SMEM((NDOC,), jnp.int32),
            pltpu.VMEM(queries.shape, jnp.bfloat16),
            pltpu.VMEM(keys.shape, jnp.bfloat16),
            pltpu.VMEM(values.shape, jnp.bfloat16),
            pltpu.SemaphoreType.DMA((6,)),
        ],
        compiler_params=pltpu.CompilerParams(vmem_limit_bytes=24 << 20),
        name="pack",
    )(*here)
    data = lax.all_to_all(packed, "ctx", 0, 0, tiled=True, axis_index_groups=[ORDER])
    other = lax.ppermute(data[:, TOK:], "ctx", [(i, i ^ 1) for i in range(CTX)])
    sums, peaks, totals = pl.pallas_call(
        own_kernel,
        out_shape=(
            jax.ShapeDtypeStruct((CTX, HEAD, TOK), jnp.float32),
            jax.ShapeDtypeStruct((CTX, TOK), jnp.float32),
            jax.ShapeDtypeStruct((CTX, TOK), jnp.float32),
        ),
        in_specs=[VMEM] * 2,
        out_specs=(VMEM,) * 3,
        compiler_params=pltpu.CompilerParams(vmem_limit_bytes=40 << 20),
        cost_estimate=pl.CostEstimate(flops=10**9, bytes_accessed=3 << 20, transcendentals=10**6),
        name="own_half",
    )(rows, data)
    mixed = pl.pallas_call(
        other_kernel,
        out_shape=jax.ShapeDtypeStruct((4, TOK, GROUP_HEADS * HEAD), jnp.bfloat16),
        in_specs=[VMEM] * 6,
        out_specs=VMEM,
        scratch_shapes=[pltpu.VMEM((4, TOK, GROUP_HEADS * HEAD), jnp.float32)],
        compiler_params=pltpu.CompilerParams(vmem_limit_bytes=40 << 20),
        name="other_half",
    )(rows, data, other, sums, peaks, totals)
    rings = [[x * 8 + y * 2 + c for y in RING] for x in range(2) for c in range(2)]
    back = lax.all_to_all(mixed, "ctx", 0, 0, tiled=True, axis_index_groups=rings)
    return pl.pallas_call(
        unpack_kernel,
        out_shape=jax.ShapeDtypeStruct(queries.shape, jnp.bfloat16),
        in_specs=[VMEM],
        out_specs=ANY,
        scratch_shapes=[pltpu.SemaphoreType.DMA((GROUPS,))],
        compiler_params=pltpu.CompilerParams(vmem_limit_bytes=16 << 20),
        name="unpack",
    )(back)


def solution(mesh):
    placed = (
        P(("dp", "ctx"), "head"),
        P(("dp", "ctx"), "head"),
        P(("dp", "ctx"), "head"),
        P("dp"),
        P("dp", None),
    )
    return jax.shard_map(
        body, mesh=mesh, in_specs=placed, out_specs=P(("dp", "ctx"), "head"), check_vma=False
    )
```

```python
import math

import jax
import jax.numpy as jnp
from jax import lax
from jax.experimental import pallas as pl
from jax.experimental.pallas import tpu as pltpu
from jax.sharding import PartitionSpec as P

HEAD = 128
CTX = 16
TOK = 128
BR = 8
NDOC = 16
GROUPS = 4
GROUP_HEADS = 4
PART = 32
REACH = 8
CHUNK = 256
MASKED = -1e30
ORDER = [5, 6, 10, 11, 8, 4, 7, 0, 1, 15, 2, 3, 13, 14, 9, 12]
PLACE = [ORDER.index(i) for i in range(CTX)]
RING = [2, 0, 3, 1]
SPOT = [RING.index(y) for y in range(4)]
SCALE = math.log2(math.e) / math.sqrt(HEAD)
ROWS_BY_ROWS = (((1,), (1,)), ((), ()))
ROWS_BY_COLS = (((1,), (0,)), ((), ()))


def dot(a, b, dims):
    return lax.dot_general(a, b, dims, preferred_element_type=jnp.float32)


def pack_kernel(owner_any, doc_any, q_any, k_any, v_any, out_ref, rows_ref, owners_ref, doc_ref, q_ref, k_ref, v_ref, sems):
    me = lax.axis_index("ctx")
    moves = (
        (owner_any, owners_ref),
        (doc_any, doc_ref),
        (k_any, k_ref),
        (v_any, v_ref),
        (q_any, q_ref),
    )
    copies = [pltpu.make_async_copy(src, dst, sems.at[i]) for i, (src, dst) in enumerate(moves)]
    for copy in copies:
        copy.start()
    for copy in copies[:2]:
        copy.wait()
    own_row = owners_ref[pl.ds(me, 1), :]
    one_lane = lax.broadcasted_iota(jnp.int32, (1, TOK), 1)
    goal = one_lane % BR
    for b in range(CTX):
        owner = own_row[:, b : b + 1]
        rank = ((owner // 8) * 2 + owner % 2) * 4 + (owner // 2) % 4
        goal = goal + jnp.where(one_lane // BR == b, rank * BR, 0)
    row = lax.broadcasted_iota(jnp.int32, (TOK, TOK), 0)
    order = jnp.where(row == goal, 1.0, 0.0).astype(jnp.bfloat16)

    lane = lax.broadcasted_iota(jnp.int32, (CTX, TOK), 1)
    shard = lax.broadcasted_iota(jnp.int32, (CTX, TOK), 0)
    mine = (me // 8) * 8 + ((lane // BR) % 4) * 2 + me % 2
    owners = owners_ref[...]
    pos = shard * TOK + lane % BR
    for b in range(CTX):
        pos = pos + jnp.where(owners[:, b : b + 1] == mine, b * BR, 0)
    start = jnp.zeros((CTX, TOK), jnp.int32)
    end = jnp.int32(0)
    for n in range(NDOC - 1):
        end = end + doc_ref[n]
        start = jnp.where(pos >= end, end, start)
    rows_ref[0] = pos
    rows_ref[1] = start

    for copy in copies[2:4]:
        copy.wait()
    for g in range(GROUPS):
        cols = slice(g * HEAD, (g + 1) * HEAD)
        keys = k_ref[:, cols]
        vals = v_ref[:, cols]
        for part in range(4):
            dest = PLACE[(part // 2) * 8 + g * 2 + part % 2]
            half = slice(part % 2 * 64, part % 2 * 64 + 64)
            out_ref[dest, 128:192, :] = keys[half]
            out_ref[dest, 192:256, :] = vals[half]
    copies[4].wait()
    for g in range(GROUPS):
        wide = slice(g * GROUP_HEADS * HEAD, (g + 1) * GROUP_HEADS * HEAD)
        moved = dot(order, q_ref[:, wide], ROWS_BY_COLS).astype(jnp.bfloat16)
        for part in range(4):
            dest = PLACE[(part // 2) * 8 + g * 2 + part % 2]
            for h in range(GROUP_HEADS):
                out_ref[dest, h * PART : (h + 1) * PART, :] = moved[
                    part * PART : (part + 1) * PART, h * HEAD : (h + 1) * HEAD
                ]


def attend_half(second, rows_ref, data_ref, half_ref, offset, sums_ref, peaks_ref, totals_ref, emit):
    half = (lax.axis_index("ctx") + second) % 2
    row = lax.broadcasted_iota(jnp.int32, (TOK, TOK), 0)
    key_at = (row // 64) * TOK + row % 64 + half * 64

    def two(ref, m, low, high):
        return jnp.concatenate([ref[PLACE[2 * m], low:high, :], ref[PLACE[2 * m + 1], low:high, :]], 0)

    def keys(m):
        return two(half_ref, m, offset, offset + 64)

    def values(m):
        return two(half_ref, m, offset + 64, offset + 128).T

    turned = [values(m) for m in range(CTX // 2)]

    def reached(pair, m, i):
        if m == pair and i == 0:
            return slice(0, 64)
        if m == pair - REACH // 2 and i == 1:
            return slice(64, TOK)
        return slice(0, TOK)

    def scores(pair):
        tiles = range(max(0, pair - REACH // 2), pair + 1)
        q = two(data_ref, pair, 0, 128)
        kept = []
        peak = [None, None]
        for m in tiles:
            both = dot(keys(m), q, ROWS_BY_ROWS)
            ones = []
            for i in range(2):
                s = 2 * pair + i
                part = reached(pair, m, i)
                one = both[part, i * TOK : (i + 1) * TOK]
                seen = key_at[part] >= rows_ref[1, s : s + 1, :] - m * 2 * TOK
                if m == pair:
                    seen = seen & (key_at[part] <= rows_ref[0, s : s + 1, :] - m * 2 * TOK)
                one = jnp.where(seen, one, MASKED)
                ones.append(one)
                top = jnp.max(one.reshape(-1, 8, TOK), axis=0)
                peak[i] = top if peak[i] is None else jnp.maximum(peak[i], top)
            kept.append(ones)
        return pair, tiles, kept, peak

    def finish(state):
        pair, tiles, kept, peak = state
        tops, totals = [], []
        for i in range(2):
            top = jnp.max(peak[i], axis=0, keepdims=True) * SCALE
            if second:
                top = jnp.maximum(top, peaks_ref[2 * pair + i : 2 * pair + i + 1, :])
            tops.append(top)
            totals.append(jnp.zeros((8, TOK), jnp.float32))
        wide = []
        none = jnp.zeros((64, TOK), jnp.bfloat16)
        for m, ones in zip(tiles, kept):
            parts = []
            for i in range(2):
                w = jnp.exp2(ones[i] * SCALE - tops[i])
                totals[i] = totals[i] + jnp.sum(w.reshape(-1, 8, TOK), axis=0)
                w = w.astype(jnp.bfloat16)
                part = reached(pair, m, i)
                if part.start > 0:
                    w = jnp.concatenate([none, w], 0)
                if part.stop < TOK:
                    w = jnp.concatenate([w, none], 0)
                parts.append(w)
            wide.append(jnp.concatenate(parts, 1))
        mixed = dot(
            jnp.concatenate([turned[m] for m in tiles], 1), jnp.concatenate(wide, 0), ROWS_BY_COLS
        )
        emit(
            pair,
            [mixed[:, i * TOK : (i + 1) * TOK] for i in range(2)],
            tops,
            [jnp.sum(total, axis=0, keepdims=True) for total in totals],
        )

    order = (1, 3, 5, 7, 6, 4, 2, 0)
    ahead = scores(order[0])
    for pair in order[1:]:
        following = scores(pair)
        finish(ahead)
        ahead = following
    finish(ahead)


def own_kernel(rows_ref, data_ref, sums_ref, peaks_ref, totals_ref):
    def emit(pair, mixed, tops, totals):
        for i in range(2):
            s = 2 * pair + i
            sums_ref[s] = mixed[i]
            peaks_ref[s : s + 1, :] = tops[i]
            totals_ref[s : s + 1, :] = totals[i]

    attend_half(0, rows_ref, data_ref, data_ref, TOK, None, None, None, emit)


def other_kernel(rows_ref, data_ref, other_ref, sums_ref, peaks_ref, totals_ref, out_ref):
    def emit(pair, mixed, tops, totals):
        rows = []
        for i in range(2):
            s = 2 * pair + i
            shrink = jnp.exp2(peaks_ref[s : s + 1, :] - tops[i])
            scale = 1.0 / (totals[i] + totals_ref[s : s + 1, :] * shrink)
            rows.append((mixed[i] * scale + sums_ref[s] * (shrink * scale)).T)
        for h in range(GROUP_HEADS):
            for y in range(4):
                at = h * PART + y * BR
                both = jnp.concatenate([rows[0][at : at + BR], rows[1][at : at + BR]], 0)
                out_ref[SPOT[y], pair * 16 : pair * 16 + 16, h * HEAD : (h + 1) * HEAD] = both.astype(jnp.bfloat16)

    attend_half(1, rows_ref, data_ref, other_ref, 0, sums_ref, peaks_ref, totals_ref, emit)


def unpack_kernel(in_ref, out_any, sems):
    wide = GROUP_HEADS * HEAD
    copies = [
        pltpu.make_async_copy(in_ref.at[SPOT[g]], out_any.at[:, g * wide : (g + 1) * wide], sems.at[g])
        for g in range(GROUPS)
    ]
    for copy in copies:
        copy.start()
    for copy in copies:
        copy.wait()


VMEM = pl.BlockSpec(memory_space=pltpu.VMEM)
ANY = pl.BlockSpec(memory_space=pl.ANY)


def body(queries, keys, values, doc_lengths, owner_map):
    here = [
        pltpu.with_memory_space_constraint(a, pltpu.HBM)
        for a in (owner_map, doc_lengths, queries, keys, values)
    ]
    packed, rows = pl.pallas_call(
        pack_kernel,
        out_shape=(
            jax.ShapeDtypeStruct((CTX, CHUNK, HEAD), jnp.bfloat16),
            jax.ShapeDtypeStruct((2, CTX, TOK), jnp.int32),
        ),
        in_specs=[ANY] * 5,
        out_specs=(VMEM, VMEM),
        scratch_shapes=[
            pltpu.VMEM((CTX, CTX), jnp.int32),
            pltpu.SMEM((NDOC,), jnp.int32),
            pltpu.VMEM(queries.shape, jnp.bfloat16),
            pltpu.VMEM(keys.shape, jnp.bfloat16),
            pltpu.VMEM(values.shape, jnp.bfloat16),
            pltpu.SemaphoreType.DMA((5,)),
        ],
        compiler_params=pltpu.CompilerParams(vmem_limit_bytes=24 << 20),
        name="pack",
    )(*here)
    data = lax.all_to_all(packed, "ctx", 0, 0, tiled=True, axis_index_groups=[ORDER])
    other = lax.ppermute(data[:, TOK:], "ctx", [(i, i ^ 1) for i in range(CTX)])
    sums, peaks, totals = pl.pallas_call(
        own_kernel,
        out_shape=(
            jax.ShapeDtypeStruct((CTX, HEAD, TOK), jnp.float32),
            jax.ShapeDtypeStruct((CTX, TOK), jnp.float32),
            jax.ShapeDtypeStruct((CTX, TOK), jnp.float32),
        ),
        in_specs=[VMEM] * 2,
        out_specs=(VMEM,) * 3,
        compiler_params=pltpu.CompilerParams(vmem_limit_bytes=40 << 20),
        cost_estimate=pl.CostEstimate(flops=10**9, bytes_accessed=3 << 20, transcendentals=10**6),
        name="own_half",
    )(rows, data)
    mixed = pl.pallas_call(
        other_kernel,
        out_shape=jax.ShapeDtypeStruct((4, TOK, GROUP_HEADS * HEAD), jnp.bfloat16),
        in_specs=[VMEM] * 6,
        out_specs=VMEM,
        compiler_params=pltpu.CompilerParams(vmem_limit_bytes=40 << 20),
        name="other_half",
    )(rows, data, other, sums, peaks, totals)
    rings = [[x * 8 + y * 2 + c for y in RING] for x in range(2) for c in range(2)]
    back = lax.all_to_all(mixed, "ctx", 0, 0, tiled=True, axis_index_groups=rings)
    return pl.pallas_call(
        unpack_kernel,
        out_shape=jax.ShapeDtypeStruct(queries.shape, jnp.bfloat16),
        in_specs=[VMEM],
        out_specs=ANY,
        scratch_shapes=[pltpu.SemaphoreType.DMA((GROUPS,))],
        compiler_params=pltpu.CompilerParams(vmem_limit_bytes=16 << 20),
        name="unpack",
    )(back)


def solution(mesh):
    placed = (
        P(("dp", "ctx"), "head"),
        P(("dp", "ctx"), "head"),
        P(("dp", "ctx"), "head"),
        P("dp"),
        P("dp", None),
    )
    return jax.shard_map(
        body, mesh=mesh, in_specs=placed, out_specs=P(("dp", "ctx"), "head"), check_vma=False
    )
```
